256 devices in a mesh: sect: 2 (over z_lo), dp: 32 (over z_hi, x, core), tp: 4 (over y).
Axes of the slice: x: 4, y: 4, z: 8 (z_hi: 4, z_lo: 2; z = z_hi * 2 + z_lo), core: 2. Of those that a mesh axis runs over, the one named last changes fastest.
Arguments:
- w_key: bfloat16 [8192, 1024], P(('sect', 'dp', 'tp')), may hold values from -0.0625 to 0.0625
- w_value: bfloat16 [8192, 1024], P(('sect', 'dp', 'tp')), may hold values from -0.0625 to 0.0625
- hidden: bfloat16 [256, 16, 8192], P(('sect', 'dp'), None, 'tp'), may hold values from -6 to 6
- queries: bfloat16 [256, 16, 8192], P(('sect', 'dp'), None, 'tp'), may hold values from -36 to 36
- key_cache: bfloat16 [256, 512, 1024], P(('sect', 'dp'), None, 'tp'), may hold values from -6 to 6
- value_cache: bfloat16 [256, 512, 1024], P(('sect', 'dp'), None, 'tp'), may hold values from -6 to 6
- prompt_lengths: int32 [256], P(('sect', 'dp')), may hold values from 64 to 512
- rollout_lengths: int32 [256], P(('sect', 'dp')), may hold values from 1 to 16
- batch_slots: int32 [256], replicated, may hold values from 0 to 255, as said below
Outputs:
- batched: bfloat16 [256, 16, 8192], P(('sect', 'dp'), None, 'tp')
The draws below stay inside these ranges and needn't reach their ends.
Inputs may be any that keep to these rules, and one draw needn't show every extreme that they name: `batch_slots`: every row number appears once; a holder owns 4 consecutive rows of the micro-batch order, and the 4 sequences of one index of sect and dp go to 4 different holders.
All inputs are finite; a program needn't handle non-finite values.
Results may differ from the reference program's by a relative error of at most 0.0059.
Values may be sent and summed in bfloat16 or wider, within the bound.
A program may use at most 64 MiB of HBM per device.

```python
import math
import jax
import jax.numpy as jnp
from jax import lax

D = 8192
QH = 64
KVH = 8
HEAD = 128
STEPS = 16
SEQ_DEV = 4
CTX = 512
SEQS = 256
KVW = 1024
GROUP = 8


def planting(key):
    signs = jax.random.randint(jax.random.fold_in(key, 11), (SEQS, HEAD), 0, 2).astype(jnp.float32) * 2.0 - 1.0
    heads = jax.random.randint(jax.random.fold_in(key, 12), (SEQS,), 0, QH)
    slots = jax.random.randint(jax.random.fold_in(key, 13), (SEQS,), 0, CTX // 8 - 1)
    dropped = jax.random.randint(jax.random.fold_in(key, 14), (SEQS,), 0, HEAD)
    levels = jax.random.randint(jax.random.fold_in(key, 15), (SEQS,), 0, 4)
    return (signs, heads, slots, dropped, levels)


def draw_key_cache(key, part):
    signs, heads, slots, dropped, levels = planting(key)
    key = jax.random.fold_in(key, 3)
    base = jnp.clip(jax.random.normal(key, (SEQS, CTX, KVW), jnp.float32), -6.0, 6.0)
    columns = jnp.arange(KVW)
    within = columns % HEAD
    in_head = (columns // HEAD)[None, :] == (heads // GROUP)[:, None]
    first = signs[:, within]
    second = jnp.where(within[None, :] == dropped[:, None], 0.0, first)
    rows = jnp.arange(CTX)
    first_row = rows[None, :] == slots[:, None]
    second_row = rows[None, :] == slots[:, None] + 1
    planted = jnp.where(first_row[:, :, None], first[:, None, :], second[:, None, :])
    chosen = in_head[:, None, :] & (first_row | second_row)[:, :, None]
    return jnp.where(chosen, planted, base).astype(jnp.bfloat16)


def draw_queries(key, part):
    signs, heads, slots, dropped, levels = planting(key)
    key = jax.random.fold_in(key, 5)
    shape = (SEQS, STEPS, QH * HEAD)
    base = jnp.clip(2.0 * jax.random.normal(key, shape, jnp.float32), -12.0, 12.0)
    strength = jnp.where(levels == 0, 1.1, jnp.where(levels == 1, 1.8, jnp.where(levels == 2, 2.5, 2.9))) * math.sqrt(HEAD)
    columns = jnp.arange(QH * HEAD)
    planted = signs[:, columns % HEAD] * strength[:, None]
    in_head = (columns // HEAD)[None, :] == heads[:, None]
    first_step = jnp.arange(STEPS) == 0
    chosen = in_head[:, None, :] & first_step[None, :, None]
    return jnp.where(chosen, planted[:, None, :], base).astype(jnp.bfloat16)


def draw_batch_slots(key, part):
    key = jax.random.fold_in(key, 7)
    holders_all = SEQS // SEQ_DEV
    order_key, shift_key, offset_key, place_key = jax.random.split(key, 4)
    sigma = jax.random.permutation(order_key, holders_all)
    tau = jax.random.permutation(shift_key, holders_all)
    offsets = jax.random.permutation(offset_key, holders_all)[:SEQ_DEV]
    holder = sigma[(tau[:, None] + offsets[None, :]) % holders_all]
    place_keys = jax.random.split(place_key, holders_all)
    places = jax.vmap(lambda k: jax.random.permutation(k, SEQ_DEV))(place_keys)
    within = places[holder, jnp.arange(SEQ_DEV)[None, :]]
    return (holder * SEQ_DEV + within).reshape(SEQS).astype(jnp.int32)


def plant(entries, own_key, smallest, high):
    longest = entries.shape.index(max(entries.shape))
    spots = []
    for shift in (0, 1):
        where = [jax.random.randint(jax.random.fold_in(own_key, axis), (), 0, length) for axis, length in enumerate(entries.shape)]
        where[longest] = (where[longest] + shift) % entries.shape[longest]
        spots.append(tuple(where))
    return entries.at[spots[0]].set(smallest).at[spots[1]].set(high)


def steps_of(rng, extent, pieces, low, top_value):
    def one(dim, parts):
        steps = jax.random.uniform(jax.random.fold_in(jax.random.fold_in(rng, 6), dim), (parts,), jnp.float32, low / len(pieces), top_value / len(pieces))
        return jnp.repeat(jnp.exp(steps), extent[dim] // parts).reshape((-1,) + (1,) * (len(extent) - dim - 1))

    gain = one(*pieces[0])
    for cut in pieces[1:]:
        gain = gain * one(*cut)
    return gain


def centred(stream_key, extent, spread, reach, shards=(), held_as=jnp.bfloat16):
    values = spread * jax.random.normal(stream_key, extent, jnp.float32)
    if shards:
        values = values * steps_of(stream_key, extent, shards, -0.22, 0.18)
    return jnp.clip(values, -reach, reach).astype(held_as)


def setup_inputs(seed: int = 0) -> dict:
    streams_of = jax.random.split(jax.random.key(seed), 10)
    return {
        "w_key": centred(streams_of[0], (D, KVW), D ** -0.5, 0.0625, ((0, 256),)),
        "w_value": centred(streams_of[1], (D, KVW), D ** -0.5, 0.0625, ((0, 256),)),
        "hidden": centred(streams_of[2], (SEQS, STEPS, D), 1.0, 6.0, ((0, 64), (2, 4))),
        "queries": draw_queries(jax.random.fold_in(streams_of[9], 71), 0),
        "key_cache": draw_key_cache(jax.random.fold_in(streams_of[9], 71), 0),
        "value_cache": centred(streams_of[5], (SEQS, CTX, KVW), 1.0, 6.0, ((0, 64), (2, 4))),
        "prompt_lengths": plant(jax.random.randint(streams_of[6], (SEQS,), CTX // 8, CTX + 1), jax.random.fold_in(streams_of[6], 1), CTX // 8, CTX).astype(jnp.int32),
        "rollout_lengths": plant(jax.random.randint(streams_of[7], (SEQS,), 1, STEPS + 1), jax.random.fold_in(streams_of[7], 1), 1, STEPS).astype(jnp.int32),
        "batch_slots": draw_batch_slots(jax.random.fold_in(streams_of[9], 71), 0),
    }


def attend(queries, new_keys, new_values, key_cache, value_cache, prompt_lengths, rollout_lengths):
    count = queries.shape[0]
    scale = HEAD ** -0.5
    query = queries.astype(jnp.float32).reshape(count, STEPS, KVH, GROUP, HEAD)
    cache_k = key_cache.astype(jnp.float32).reshape(count, CTX, KVH, HEAD)
    cache_v = value_cache.astype(jnp.float32).reshape(count, CTX, KVH, HEAD)
    fresh_k = new_keys.astype(jnp.float32).reshape(count, STEPS, KVH, HEAD)
    fresh_v = new_values.astype(jnp.float32).reshape(count, STEPS, KVH, HEAD)
    live = (jnp.arange(CTX)[None, :] < prompt_lengths[:, None])[:, None, None, None, :]
    causal = (jnp.arange(STEPS)[None, :] <= jnp.arange(STEPS)[:, None])[None, :, None, None, :]
    score_c = jnp.einsum("nikgd,njkd->nikgj", query, cache_k) * scale
    score_n = jnp.einsum("nikgd,njkd->nikgj", query, fresh_k) * scale
    score_c = jnp.where(live, score_c, -1e30)
    score_n = jnp.where(causal, score_n, -1e30)
    top = jnp.maximum(jnp.max(score_c, axis=-1), jnp.max(score_n, axis=-1))
    exp_c = jnp.exp(score_c - top[..., None])
    exp_n = jnp.exp(score_n - top[..., None])
    total = jnp.sum(exp_c, axis=-1) + jnp.sum(exp_n, axis=-1)
    weight_c = (exp_c / total[..., None]).astype(jnp.bfloat16).astype(jnp.float32)
    weight_n = (exp_n / total[..., None]).astype(jnp.bfloat16).astype(jnp.float32)
    result = jnp.einsum("nikgj,njkd->nikgd", weight_c, cache_v) + jnp.einsum("nikgj,njkd->nikgd", weight_n, fresh_v)
    keep = (jnp.arange(STEPS)[None, :] < rollout_lengths[:, None])[:, :, None, None, None]
    result = jnp.where(keep, result, 0.0)
    return result.astype(jnp.bfloat16).reshape(count, STEPS, QH * HEAD)


def reference(w_key, w_value, hidden, queries, key_cache, value_cache, prompt_lengths, rollout_lengths, batch_slots):
    flat = hidden.reshape(SEQS * STEPS, D)
    new_keys = jnp.dot(flat, w_key, preferred_element_type=jnp.float32).astype(jnp.bfloat16).reshape(SEQS, STEPS, KVW)
    new_values = jnp.dot(flat, w_value, preferred_element_type=jnp.float32).astype(jnp.bfloat16).reshape(SEQS, STEPS, KVW)
    blocks = SEQS // 8

    def split(a):
        return a.reshape((blocks, 8) + a.shape[1:])

    def one_block(items):
        return attend(*items)

    attended = lax.map(one_block, (split(queries), split(new_keys), split(new_values), split(key_cache), split(value_cache), split(prompt_lengths), split(rollout_lengths)))
    attended = attended.reshape(SEQS, STEPS, QH * HEAD)
    return jnp.zeros_like(attended).at[batch_slots].set(attended)
```

```python
import functools

import jax
import jax.numpy as jnp
from jax import lax
from jax.experimental import pallas as pl
from jax.experimental.pallas import tpu as pltpu
from jax.sharding import PartitionSpec as P

MESH = pl.DeviceIdType.MESH
HEAD = 128
STEPS = 16
CTX = 512
GROUP = 8
SEQ = 4
TOK = SEQ * STEPS
NX, NY, NZ = 4, 4, 8
HOLDERS = 64
LOG2E = 1.4426950408889634
NEG = -1e30


def kernel(
    lens, rolls, slots, w_key, w_value, hidden, queries, key_cache, value_cache, out,
    acts, weights, qs, kc, vc, part, part_send, part_recv, fresh, qrows, oc, mc, lc, pick,
    send_a, recv_a, send_b, recv_b, wide_a, wide_b,
    loc, w1s, w1r, h1s, h1r, ups, upr, dns, dnr, fus, fur, fds, fdr,
    zus, zur, zds, zdr, cs, cr, rs, rr, a_s, a_r, b_s, b_r,
):
    sect, dp, tp = lax.axis_index("sect"), lax.axis_index("dp"), lax.axis_index("tp")
    z_hi, x, core = dp // 8, (dp // 2) % 4, dp % 2
    z = 2 * z_hi + sect
    me = sect * 32 + dp

    def at_z(d):
        return (z + d + NZ) % NZ

    def block(zp):
        return (zp % 2) * 4 + zp // 2

    def device(dx=0, dy=0, dz=0, other=False):
        zp = at_z(dz)
        c = 1 - core if other else core
        return (zp % 2, (zp // 2) * 8 + ((x + dx + NX) % NX) * 2 + c, (tp + dy + NY) % NY)

    started = []

    def send(src, dst, s_sem, r_sem, to):
        copy = pltpu.make_async_remote_copy(
            src_ref=src, dst_ref=dst, send_sem=s_sem, recv_sem=r_sem, device_id=to, device_id_type=MESH
        )
        copy.start()
        started.append(copy)
        return copy

    def local(src, dst, sem):
        copy = pltpu.make_async_copy(src, dst, sem)
        copy.start()
        return copy

    zz = block(z)
    rows_w = pl.ds(pl.multiple_of(core * 128 + tp * 32, 32), 32)

    def cols(y):
        return pl.ds(pl.multiple_of(y * 256, 256), 256)

    w1 = []
    for k in range(1, NY):
        y = (tp + k) % NY
        w1.append(
            [
                send(w_key.at[:, cols(y)], weights.at[zz, rows_w, 0:256], w1s.at[k - 1, 0], w1r.at[k - 1, 0], device(dy=k)),
                send(w_value.at[:, cols(y)], weights.at[zz, rows_w, 256:512], w1s.at[k - 1, 1], w1r.at[k - 1, 1], device(dy=k)),
            ]
        )
    own_w = [
        local(w_key.at[:, cols(tp)], weights.at[zz, rows_w, 0:256], loc.at[0]),
        local(w_value.at[:, cols(tp)], weights.at[zz, rows_w, 256:512], loc.at[1]),
    ]
    my_rows = pl.ds(pl.multiple_of(x * TOK, TOK), TOK)

    def feats(half, xp):
        return pl.ds(pl.multiple_of(half * 1024 + xp * 256, 256), 256)

    h1 = {}
    for k in (1, 3, 2):
        to = (x + k) % NX
        h1[k] = [
            send(hidden.at[:, feats(b, to)], acts.at[tp, my_rows, b * 256 : b * 256 + 256], h1s.at[k - 1, b], h1r.at[k - 1, b], device(dx=k))
            for b in range(2)
        ]
    own_h = [
        local(hidden.at[:, feats(b, x)], acts.at[tp, my_rows, b * 256 : b * 256 + 256], loc.at[2 + b])
        for b in range(2)
    ]
    own_q = [local(queries, qs, loc.at[4]), local(key_cache, kc, loc.at[5]), local(value_cache, vc, loc.at[6])]

    def chunk(d, h):
        return weights.at[block(at_z(d)), pl.ds(pl.multiple_of(core * 128 + h * 64, 64), 64), :]

    up, down, across = {}, {}, []

    def zsend(step, h, direction):
        if direction > 0:
            ref = chunk(-(step - 1), h)
            up[step, h] = send(ref, ref, zus.at[step - 1, h], zur.at[step - 1, h], device(dz=1))
        else:
            ref = chunk(step - 1, h)
            down[step, h] = send(ref, ref, zds.at[step - 1, h], zdr.at[step - 1, h], device(dz=-1))

    def to_core(d, h):
        ref = chunk(d, h)
        across.append(send(ref, ref, cs.at[d % NZ, h], cr.at[d % NZ, h], device(other=True)))

    def zstep(step, h):
        up[step, h].wait_recv()
        if step < 3 or h == 0:
            zsend(step + 1, h, 1)
        down[step, h].wait_recv()
        if step < 3 or h == 1:
            zsend(step + 1, h, -1)
        to_core(-step, h)
        to_core(step, h)

    for pair in w1:
        for copy in pair:
            copy.wait_recv()
    for copy in own_w:
        copy.wait()
    for h in range(2):
        zsend(1, h, 1)
        zsend(1, h, -1)
    for h in range(2):
        to_core(0, h)

    def rows_of(k):
        return pl.ds(pl.multiple_of(((x - k + NX) % NX) * TOK, TOK), TOK)

    hup, hdn, hfu, hfd = {}, {}, {}, {}

    def ysend(k):
        ref = acts.at[tp, rows_of(k), :]
        hup[k] = send(ref, ref, ups.at[k], upr.at[k], device(dy=1))
        hdn[k] = send(ref, ref, dns.at[k], dnr.at[k], device(dy=-1))

    def yforward(k):
        if k % 2 == 0:
            hup[k].wait_recv()
            ref = acts.at[(tp + NY - 1) % NY, rows_of(k), :]
            hfu[k] = send(ref, ref, fus.at[k // 2], fur.at[k // 2], device(dy=1))
        else:
            hdn[k].wait_recv()
            ref = acts.at[(tp + 1) % NY, rows_of(k), :]
            hfd[k] = send(ref, ref, fds.at[k // 2], fdr.at[k // 2], device(dy=-1))

    for copy in own_h:
        copy.wait()
    ysend(0)
    for k in (1, 3, 2):
        for copy in h1[k]:
            copy.wait_recv()
        ysend(k)

    scale = HEAD ** (-0.5) * LOG2E

    def over_cache(n, kv):
        q = jnp.concatenate(
            [qs[n * STEPS : (n + 1) * STEPS, (kv * GROUP + g) * HEAD : (kv * GROUP + g + 1) * HEAD] for g in range(GROUP)],
            axis=0,
        )
        rows = slice(n * 128, (n + 1) * 128)
        qrows[kv, rows, :] = q
        keys = kc[n * CTX : (n + 1) * CTX, kv * HEAD : (kv + 1) * HEAD]
        vals = vc[n * CTX : (n + 1) * CTX, kv * HEAD : (kv + 1) * HEAD]
        score = lax.dot_general(q, keys, (((1,), (1,)), ((), ())), preferred_element_type=jnp.float32)
        live = lax.broadcasted_iota(jnp.int32, (128, CTX), 1) < lens[n]
        score = jnp.where(live, score * scale, NEG)
        top = jnp.max(score, axis=1, keepdims=True)
        e = jnp.exp2(score - top)
        total = jnp.sum(e, axis=1, keepdims=True)
        oc[kv, rows, :] = jnp.dot(e.astype(jnp.bfloat16), vals, preferred_element_type=jnp.float32)
        mc[kv, rows, :] = jnp.broadcast_to(top, (128, HEAD))
        lc[kv, rows, :] = jnp.broadcast_to(total, (128, HEAD))

    row = lax.broadcasted_iota(jnp.int32, (256, 256), 0)
    pick[...] = jnp.where(row == slots[...], 1.0, 0.0).astype(jnp.bfloat16)

    zstep(1, 0)
    yforward(0)
    zstep(1, 1)
    yforward(1)
    for copy in own_q:
        copy.wait()
    over_cache(0, 0)
    yforward(3)
    zstep(2, 0)
    yforward(2)
    over_cache(0, 1)
    zstep(2, 1)
    over_cache(1, 0)
    zstep(3, 0)
    over_cache(1, 1)
    zstep(3, 1)
    over_cache(2, 0)
    over_cache(2, 1)
    up[4, 0].wait_recv()
    to_core(4, 0)
    down[4, 1].wait_recv()
    to_core(4, 1)
    over_cache(3, 0)
    over_cache(3, 1)
    for k in (1, 3):
        hup[k].wait_recv()
    for k in (0, 2):
        hdn[k].wait_recv()
    for copy in list(hfu.values()) + list(hfd.values()) + across:
        copy.wait_recv()

    total = None
    for y in range(NY):
        term = jnp.dot(
            acts[y], weights[2 * y : 2 * y + 2].reshape(512, 512), preferred_element_type=jnp.float32
        )
        total = term if total is None else total + term
    part[...] = total.reshape(NX, TOK, 512)
    part_send[...] = total.reshape(NX, TOK, 512).astype(jnp.bfloat16)
    sums = [
        send(part_send.at[(x + k) % NX], part_recv.at[k - 1], rs.at[k - 1], rr.at[k - 1], device(dx=k))
        for k in (1, 3, 2)
    ]
    for copy in sums:
        copy.wait_recv()
    both = part[x]
    for k in range(3):
        both = both + part_recv[k].astype(jnp.float32)
    fresh[...] = both.astype(jnp.bfloat16)

    r = lax.broadcasted_iota(jnp.int32, (512, TOK), 0)
    j = lax.broadcasted_iota(jnp.int32, (512, TOK), 1)
    seen = (r // 128 == j // STEPS) & (j % STEPS <= r % STEPS)
    step = lax.broadcasted_iota(jnp.int32, (128, HEAD), 0) % STEPS
    for kv in range(2):
        keys = fresh[:, kv * HEAD : (kv + 1) * HEAD]
        vals = fresh[:, 256 + kv * HEAD : 256 + (kv + 1) * HEAD]
        score = lax.dot_general(qrows[kv], keys, (((1,), (1,)), ((), ())), preferred_element_type=jnp.float32)
        score = jnp.where(seen, score * scale, NEG)
        old = mc[kv]
        top = jnp.maximum(old, jnp.broadcast_to(jnp.max(score, axis=1, keepdims=True), (512, HEAD)))
        e = jnp.exp2(score - top[:, :TOK])
        shrink = jnp.exp2(old - top)
        denom = lc[kv] * shrink + jnp.broadcast_to(jnp.sum(e, axis=1, keepdims=True), (512, HEAD))
        value = oc[kv] * shrink + jnp.dot(e.astype(jnp.bfloat16), vals, preferred_element_type=jnp.float32)
        value = value / denom
        for n in range(SEQ):
            oc[kv, n * 128 : (n + 1) * 128, :] = jnp.where(step < rolls[n], value[n * 128 : (n + 1) * 128], 0.0)
        for q in range(32):
            send_a[kv * 32 + q] = oc[kv, pl.ds(q, 16, stride=32), :].astype(jnp.bfloat16)

    def spread(src, dst, s_sem, r_sem):
        def one(k, carry):
            to = (me + k) % HOLDERS
            pltpu.make_async_remote_copy(
                src_ref=src.at[to], dst_ref=dst.at[me], send_sem=s_sem, recv_sem=r_sem,
                device_id=(to // 32, to % 32, tp), device_id_type=MESH,
            ).start()
            return carry

        lax.fori_loop(1, HOLDERS, one, 0)
        dst[me] = src[me]

    def arrived(buf, sem):
        some = buf.at[pl.ds(0, HOLDERS - 1)]
        pltpu.make_async_copy(some, some, sem).wait()

    spread(send_a, recv_a, a_s, a_r)
    arrived(recv_a, a_r)
    wide_a[...] = recv_a[...].reshape(1024, HEAD).astype(jnp.float32)
    for u in range(4):
        pieces = wide_a[pl.ds(u, 256, stride=4), :].astype(jnp.bfloat16)
        wide_b[pl.ds(u, 256, stride=4), :] = jnp.dot(pick[...], pieces, preferred_element_type=jnp.float32)
    send_b[...] = wide_b[...].astype(jnp.bfloat16).reshape(HOLDERS, 16, HEAD)
    spread(send_b, recv_b, b_s, b_r)
    arrived(recv_b, b_r)
    wide_a[...] = recv_b[...].reshape(1024, HEAD).astype(jnp.float32)
    for kv in range(2):
        for qh in range(2):
            for u in range(4):
                col = (kv * GROUP + 2 * u + qh) * HEAD
                for n in range(SEQ):
                    base = (kv * 2 + qh) * 256 + n * 4 + u
                    out[n * STEPS : (n + 1) * STEPS, col : col + HEAD] = wide_a[
                        pl.ds(base, 16, stride=16), :
                    ].astype(jnp.bfloat16)
    for copy in started:
        copy.wait_send()
    arrived(send_a, a_s)
    arrived(send_b, b_s)


def shards(
    w_key, w_value, hidden, queries, key_cache, value_cache, prompt_lengths, rollout_lengths, batch_slots
):
    bf, f32 = jnp.bfloat16, jnp.float32
    vm, dma = pltpu.VMEM, pltpu.SemaphoreType.DMA
    hbm = pl.BlockSpec(memory_space=pl.ANY)
    smem = pl.BlockSpec(memory_space=pltpu.SMEM)
    vmem = pl.BlockSpec(memory_space=pltpu.VMEM)
    scratch = [
        vm((NY, NX * TOK, 512), bf),
        vm((NZ, 256, 512), bf),
        vm((TOK, 2048), bf),
        vm((SEQ * CTX, 256), bf),
        vm((SEQ * CTX, 256), bf),
        vm((NX, TOK, 512), f32),
        vm((NX, TOK, 512), bf),
        vm((NX - 1, TOK, 512), bf),
        vm((TOK, 512), bf),
        vm((2, 512, HEAD), bf),
        vm((2, 512, HEAD), f32),
        vm((2, 512, HEAD), f32),
        vm((2, 512, HEAD), f32),
        vm((256, 256), bf),
    ]
    scratch += [vm((HOLDERS, 16, HEAD), bf)] * 4 + [vm((1024, HEAD), f32)] * 2
    scratch += [dma((7,))]
    scratch += [dma((3, 2))] * 4
    scratch += [dma((4,))] * 4 + [dma((2,))] * 4
    scratch += [dma((4, 2))] * 4 + [dma((NZ, 2))] * 2
    scratch += [dma((3,))] * 2
    scratch += [dma] * 4
    result = pl.pallas_call(
        kernel,
        out_shape=jax.ShapeDtypeStruct((TOK, 2048), bf),
        in_specs=[smem, smem, vmem] + [hbm] * 6,
        out_specs=vmem,
        scratch_shapes=scratch,
        compiler_params=pltpu.CompilerParams(has_side_effects=True, vmem_limit_bytes=32 * 1024 * 1024),
        name="rollout",
    )(
        prompt_lengths,
        rollout_lengths,
        batch_slots.reshape(1, 256),
        w_key,
        w_value,
        hidden.reshape(TOK, 2048),
        queries.reshape(TOK, 2048),
        key_cache.reshape(SEQ * CTX, 256),
        value_cache.reshape(SEQ * CTX, 256),
    )
    return result.reshape(SEQ, STEPS, 2048)


def solution(mesh):
    rows = P(("sect", "dp", "tp"), None)
    spread = P(("sect", "dp"), None, "tp")
    each = P(("sect", "dp"))
    return jax.shard_map(
        shards,
        mesh=mesh,
        in_specs=(rows, rows, spread, spread, spread, spread, each, each, P()),
        out_specs=spread,
        check_vma=False,
    )
```

```python
import functools

import jax
import jax.numpy as jnp
from jax import lax
from jax.experimental import pallas as pl
from jax.experimental.pallas import tpu as pltpu
from jax.sharding import PartitionSpec as P

MESH = pl.DeviceIdType.MESH
HEAD = 128
STEPS = 16
CTX = 512
GROUP = 8
SEQ = 4
TOK = SEQ * STEPS
NX, NY, NZ = 4, 4, 8
HOLDERS = 64
LOG2E = 1.4426950408889634
NEG = -1e30


def kernel(
    lens, rolls, slots, w_key, w_value, hidden, queries, key_cache, value_cache, out,
    acts, weights, qs, kc, vc, part, part_send, part_recv, fresh, qrows, oc, mc, lc, pick,
    send_a, recv_a, send_b, recv_b, wide_a, wide_b,
    loc, w1s, w1r, h1s, h1r, ups, upr, dns, dnr, fus, fur, fds, fdr,
    zus, zur, zds, zdr, cs, cr, rs, rr, a_s, a_r, b_s, b_r,
):
    sect, dp, tp = lax.axis_index("sect"), lax.axis_index("dp"), lax.axis_index("tp")
    z_hi, x, core = dp // 8, (dp // 2) % 4, dp % 2
    z = 2 * z_hi + sect
    me = sect * 32 + dp

    def at_z(d):
        return (z + d + NZ) % NZ

    def block(zp):
        return (zp % 2) * 4 + zp // 2

    def device(dx=0, dy=0, dz=0, other=False):
        zp = at_z(dz)
        c = 1 - core if other else core
        return (zp % 2, (zp // 2) * 8 + ((x + dx + NX) % NX) * 2 + c, (tp + dy + NY) % NY)

    partners = [device(dx=k) for k in range(1, NX)] + [device(dy=k) for k in range(1, NY)]
    partners += [device(dz=1), device(dz=-1), device(other=True)]
    barrier = pltpu.get_barrier_semaphore()
    for partner in partners:
        pl.semaphore_signal(barrier, inc=1, device_id=partner, device_id_type=MESH)
    pl.semaphore_wait(barrier, len(partners))

    started = []

    def send(src, dst, s_sem, r_sem, to):
        copy = pltpu.make_async_remote_copy(
            src_ref=src, dst_ref=dst, send_sem=s_sem, recv_sem=r_sem, device_id=to, device_id_type=MESH
        )
        copy.start()
        started.append(copy)
        return copy

    def local(src, dst, sem):
        copy = pltpu.make_async_copy(src, dst, sem)
        copy.start()
        return copy

    zz = block(z)
    rows_w = pl.ds(pl.multiple_of(core * 128 + tp * 32, 32), 32)

    def cols(y):
        return pl.ds(pl.multiple_of(y * 256, 256), 256)

    w1 = []
    for k in range(1, NY):
        y = (tp + k) % NY
        w1.append(
            [
                send(w_key.at[:, cols(y)], weights.at[zz, rows_w, 0:256], w1s.at[k - 1, 0], w1r.at[k - 1, 0], device(dy=k)),
                send(w_value.at[:, cols(y)], weights.at[zz, rows_w, 256:512], w1s.at[k - 1, 1], w1r.at[k - 1, 1], device(dy=k)),
            ]
        )
    own_w = [
        local(w_key.at[:, cols(tp)], weights.at[zz, rows_w, 0:256], loc.at[0]),
        local(w_value.at[:, cols(tp)], weights.at[zz, rows_w, 256:512], loc.at[1]),
    ]
    my_rows = pl.ds(pl.multiple_of(x * TOK, TOK), TOK)

    def feats(half, xp):
        return pl.ds(pl.multiple_of(half * 1024 + xp * 256, 256), 256)

    h1 = {}
    for k in (1, 3, 2):
        to = (x + k) % NX
        h1[k] = [
            send(hidden.at[:, feats(b, to)], acts.at[tp, my_rows, b * 256 : b * 256 + 256], h1s.at[k - 1, b], h1r.at[k - 1, b], device(dx=k))
            for b in range(2)
        ]
    own_h = [
        local(hidden.at[:, feats(b, x)], acts.at[tp, my_rows, b * 256 : b * 256 + 256], loc.at[2 + b])
        for b in range(2)
    ]
    own_q = [local(queries, qs, loc.at[4]), local(key_cache, kc, loc.at[5]), local(value_cache, vc, loc.at[6])]

    def chunk(d, h):
        return weights.at[block(at_z(d)), pl.ds(pl.multiple_of(core * 128 + h * 64, 64), 64), :]

    up, down, across = {}, {}, []

    def zsend(step, h, direction):
        if direction > 0:
            ref = chunk(-(step - 1), h)
            up[step, h] = send(ref, ref, zus.at[step - 1, h], zur.at[step - 1, h], device(dz=1))
        else:
            ref = chunk(step - 1, h)
            down[step, h] = send(ref, ref, zds.at[step - 1, h], zdr.at[step - 1, h], device(dz=-1))

    def to_core(d, h):
        ref = chunk(d, h)
        across.append(send(ref, ref, cs.at[d % NZ, h], cr.at[d % NZ, h], device(other=True)))

    def zstep(step, h):
        up[step, h].wait_recv()
        if step < 3 or h == 0:
            zsend(step + 1, h, 1)
        down[step, h].wait_recv()
        if step < 3 or h == 1:
            zsend(step + 1, h, -1)
        to_core(-step, h)
        to_core(step, h)

    for pair in w1:
        for copy in pair:
            copy.wait_recv()
    for copy in own_w:
        copy.wait()
    for h in range(2):
        zsend(1, h, 1)
        zsend(1, h, -1)
    for h in range(2):
        to_core(0, h)

    def rows_of(k):
        return pl.ds(pl.multiple_of(((x - k + NX) % NX) * TOK, TOK), TOK)

    hup, hdn, hfu, hfd = {}, {}, {}, {}

    def ysend(k):
        ref = acts.at[tp, rows_of(k), :]
        hup[k] = send(ref, ref, ups.at[k], upr.at[k], device(dy=1))
        hdn[k] = send(ref, ref, dns.at[k], dnr.at[k], device(dy=-1))

    def yforward(k):
        if k % 2 == 0:
            hup[k].wait_recv()
            ref = acts.at[(tp + NY - 1) % NY, rows_of(k), :]
            hfu[k] = send(ref, ref, fus.at[k // 2], fur.at[k // 2], device(dy=1))
        else:
            hdn[k].wait_recv()
            ref = acts.at[(tp + 1) % NY, rows_of(k), :]
            hfd[k] = send(ref, ref, fds.at[k // 2], fdr.at[k // 2], device(dy=-1))

    for copy in own_h:
        copy.wait()
    ysend(0)
    for k in (1, 3, 2):
        for copy in h1[k]:
            copy.wait_recv()
        ysend(k)

    scale = HEAD ** (-0.5) * LOG2E

    def over_cache(n, kv):
        q = jnp.concatenate(
            [qs[n * STEPS : (n + 1) * STEPS, (kv * GROUP + g) * HEAD : (kv * GROUP + g + 1) * HEAD] for g in range(GROUP)],
            axis=0,
        )
        rows = slice(n * 128, (n + 1) * 128)
        qrows[kv, rows, :] = q
        keys = kc[n * CTX : (n + 1) * CTX, kv * HEAD : (kv + 1) * HEAD]
        vals = vc[n * CTX : (n + 1) * CTX, kv * HEAD : (kv + 1) * HEAD]
        score = lax.dot_general(q, keys, (((1,), (1,)), ((), ())), preferred_element_type=jnp.float32)
        live = lax.broadcasted_iota(jnp.int32, (128, CTX), 1) < lens[n]
        score = jnp.where(live, score * scale, NEG)
        top = jnp.max(score, axis=1, keepdims=True)
        e = jnp.exp2(score - top)
        total = jnp.sum(e, axis=1, keepdims=True)
        oc[kv, rows, :] = jnp.dot(e.astype(jnp.bfloat16), vals, preferred_element_type=jnp.float32)
        mc[kv, rows, :] = jnp.broadcast_to(top, (128, HEAD))
        lc[kv, rows, :] = jnp.broadcast_to(total, (128, HEAD))

    row = lax.broadcasted_iota(jnp.int32, (256, 256), 0)
    pick[...] = jnp.where(row == slots[...], 1.0, 0.0).astype(jnp.bfloat16)

    zstep(1, 0)
    yforward(0)
    zstep(1, 1)
    yforward(1)
    for copy in own_q:
        copy.wait()
    over_cache(0, 0)
    yforward(3)
    zstep(2, 0)
    yforward(2)
    over_cache(0, 1)
    zstep(2, 1)
    over_cache(1, 0)
    zstep(3, 0)
    over_cache(1, 1)
    zstep(3, 1)
    over_cache(2, 0)
    over_cache(2, 1)
    up[4, 0].wait_recv()
    to_core(4, 0)
    down[4, 1].wait_recv()
    to_core(4, 1)
    over_cache(3, 0)
    over_cache(3, 1)
    for k in (1, 3):
        hup[k].wait_recv()
    for k in (0, 2):
        hdn[k].wait_recv()
    for copy in list(hfu.values()) + list(hfd.values()) + across:
        copy.wait_recv()

    total = None
    for y in range(NY):
        term = jnp.dot(
            acts[y], weights[2 * y : 2 * y + 2].reshape(512, 512), preferred_element_type=jnp.float32
        )
        total = term if total is None else total + term
    part[...] = total.reshape(NX, TOK, 512)
    part_send[...] = total.reshape(NX, TOK, 512).astype(jnp.bfloat16)
    sums = [
        send(part_send.at[(x + k) % NX], part_recv.at[k - 1], rs.at[k - 1], rr.at[k - 1], device(dx=k))
        for k in (1, 3, 2)
    ]
    for copy in sums:
        copy.wait_recv()
    both = part[x]
    for k in range(3):
        both = both + part_recv[k].astype(jnp.float32)
    fresh[...] = both.astype(jnp.bfloat16)

    r = lax.broadcasted_iota(jnp.int32, (512, TOK), 0)
    j = lax.broadcasted_iota(jnp.int32, (512, TOK), 1)
    seen = (r // 128 == j // STEPS) & (j % STEPS <= r % STEPS)
    step = lax.broadcasted_iota(jnp.int32, (128, HEAD), 0) % STEPS
    for kv in range(2):
        keys = fresh[:, kv * HEAD : (kv + 1) * HEAD]
        vals = fresh[:, 256 + kv * HEAD : 256 + (kv + 1) * HEAD]
        score = lax.dot_general(qrows[kv], keys, (((1,), (1,)), ((), ())), preferred_element_type=jnp.float32)
        score = jnp.where(seen, score * scale, NEG)
        old = mc[kv]
        top = jnp.maximum(old, jnp.broadcast_to(jnp.max(score, axis=1, keepdims=True), (512, HEAD)))
        e = jnp.exp2(score - top[:, :TOK])
        shrink = jnp.exp2(old - top)
        denom = lc[kv] * shrink + jnp.broadcast_to(jnp.sum(e, axis=1, keepdims=True), (512, HEAD))
        value = oc[kv] * shrink + jnp.dot(e.astype(jnp.bfloat16), vals, preferred_element_type=jnp.float32)
        value = value / denom
        for n in range(SEQ):
            oc[kv, n * 128 : (n + 1) * 128, :] = jnp.where(step < rolls[n], value[n * 128 : (n + 1) * 128], 0.0)
        for q in range(32):
            send_a[kv * 32 + q] = oc[kv, pl.ds(q, 16, stride=32), :].astype(jnp.bfloat16)

    def spread(src, dst, s_sem, r_sem):
        def one(k, carry):
            to = (me + k) % HOLDERS
            pltpu.make_async_remote_copy(
                src_ref=src.at[to], dst_ref=dst.at[me], send_sem=s_sem, recv_sem=r_sem,
                device_id=(to // 32, to % 32, tp), device_id_type=MESH,
            ).start()
            return carry

        lax.fori_loop(1, HOLDERS, one, 0)
        dst[me] = src[me]

    def arrived(buf, sem):
        some = buf.at[pl.ds(0, HOLDERS - 1)]
        pltpu.make_async_copy(some, some, sem).wait()

    spread(send_a, recv_a, a_s, a_r)
    arrived(recv_a, a_r)
    wide_a[...] = recv_a[...].reshape(1024, HEAD).astype(jnp.float32)
    for u in range(4):
        pieces = wide_a[pl.ds(u, 256, stride=4), :].astype(jnp.bfloat16)
        wide_b[pl.ds(u, 256, stride=4), :] = jnp.dot(pick[...], pieces, preferred_element_type=jnp.float32)
    send_b[...] = wide_b[...].astype(jnp.bfloat16).reshape(HOLDERS, 16, HEAD)
    spread(send_b, recv_b, b_s, b_r)
    arrived(recv_b, b_r)
    wide_a[...] = recv_b[...].reshape(1024, HEAD).astype(jnp.float32)
    for kv in range(2):
        for qh in range(2):
            for u in range(4):
                col = (kv * GROUP + 2 * u + qh) * HEAD
                for n in range(SEQ):
                    base = (kv * 2 + qh) * 256 + n * 4 + u
                    out[n * STEPS : (n + 1) * STEPS, col : col + HEAD] = wide_a[
                        pl.ds(base, 16, stride=16), :
                    ].astype(jnp.bfloat16)
    for copy in started:
        copy.wait_send()
    arrived(send_a, a_s)
    arrived(send_b, b_s)


def shards(
    w_key, w_value, hidden, queries, key_cache, value_cache, prompt_lengths, rollout_lengths, batch_slots
):
    bf, f32 = jnp.bfloat16, jnp.float32
    vm, dma = pltpu.VMEM, pltpu.SemaphoreType.DMA
    hbm = pl.BlockSpec(memory_space=pl.ANY)
    smem = pl.BlockSpec(memory_space=pltpu.SMEM)
    vmem = pl.BlockSpec(memory_space=pltpu.VMEM)
    scratch = [
        vm((NY, NX * TOK, 512), bf),
        vm((NZ, 256, 512), bf),
        vm((TOK, 2048), bf),
        vm((SEQ * CTX, 256), bf),
        vm((SEQ * CTX, 256), bf),
        vm((NX, TOK, 512), f32),
        vm((NX, TOK, 512), bf),
        vm((NX - 1, TOK, 512), bf),
        vm((TOK, 512), bf),
        vm((2, 512, HEAD), bf),
        vm((2, 512, HEAD), f32),
        vm((2, 512, HEAD), f32),
        vm((2, 512, HEAD), f32),
        vm((256, 256), bf),
    ]
    scratch += [vm((HOLDERS, 16, HEAD), bf)] * 4 + [vm((1024, HEAD), f32)] * 2
    scratch += [dma((7,))]
    scratch += [dma((3, 2))] * 4
    scratch += [dma((4,))] * 4 + [dma((2,))] * 4
    scratch += [dma((4, 2))] * 4 + [dma((NZ, 2))] * 2
    scratch += [dma((3,))] * 2
    scratch += [dma] * 4
    result = pl.pallas_call(
        kernel,
        out_shape=jax.ShapeDtypeStruct((TOK, 2048), bf),
        in_specs=[smem, smem, vmem] + [hbm] * 6,
        out_specs=vmem,
        scratch_shapes=scratch,
        compiler_params=pltpu.CompilerParams(collective_id=0, has_side_effects=True, vmem_limit_bytes=60 * 1024 * 1024),
        name="rollout",
    )(
        prompt_lengths,
        rollout_lengths,
        batch_slots.reshape(1, 256),
        w_key,
        w_value,
        hidden.reshape(TOK, 2048),
        queries.reshape(TOK, 2048),
        key_cache.reshape(SEQ * CTX, 256),
        value_cache.reshape(SEQ * CTX, 256),
    )
    return result.reshape(SEQ, STEPS, 2048)


def solution(mesh):
    rows = P(("sect", "dp", "tp"), None)
    spread = P(("sect", "dp"), None, "tp")
    each = P(("sect", "dp"))
    return jax.shard_map(
        shards,
        mesh=mesh,
        in_specs=(rows, rows, spread, spread, spread, spread, each, each, P()),
        out_specs=spread,
        check_vma=False,
    )
```

```python
import functools

import jax
import jax.numpy as jnp
from jax import lax
from jax.experimental import pallas as pl
from jax.experimental.pallas import tpu as pltpu
from jax.sharding import PartitionSpec as P

MESH = pl.DeviceIdType.MESH
HEAD = 128
STEPS = 16
CTX = 512
GROUP = 8
SEQ = 4
TOK = SEQ * STEPS
NX, NY, NZ = 4, 4, 8
HOLDERS = 64
LOG2E = 1.4426950408889634
NEG = -1e30
FIRST = [(1,), (1,), (1,), (1,)]
ONWARD = [{1: (1,), 2: (1, 2)}] * 4
GREET = (-1, 1)


def kernel(
    lens, rolls, slots, w_key, w_value, hidden, queries, key_cache, value_cache, out,
    w_stage, h_stage, acts, weights, qs, kc, vc, part, part_send, part_recv, fresh, qrows, oc, mc, lc, pick,
    send_a, recv_a, send_b, recv_b, wide_a, wide_b,
    loc, w1s, w1r, h1s, h1r, ups, upr, dns, dnr, fus, fur, fds, fdr, hxs, hxr,
    zus, zur, zds, zdr, rs, rr, a_s, a_r, b_s, b_r,
):
    sect, dp, tp = lax.axis_index("sect"), lax.axis_index("dp"), lax.axis_index("tp")
    z_hi, x, core = dp // 8, (dp // 2) % 4, dp % 2
    z = 2 * z_hi + sect
    me = sect * 32 + dp

    def at_z(d):
        return (z + d + NZ) % NZ

    def block(zp):
        return (zp % 2) * 4 + zp // 2

    def device(dx=0, dy=0, dz=0, other=False):
        zp = at_z(dz)
        c = 1 - core if other else core
        return (zp % 2, (zp // 2) * 8 + ((x + dx + NX) % NX) * 2 + c, (tp + dy + NY) % NY)

    started = []

    def send(src, dst, s_sem, r_sem, to):
        copy = pltpu.make_async_remote_copy(
            src_ref=src, dst_ref=dst, send_sem=s_sem, recv_sem=r_sem, device_id=to, device_id_type=MESH
        )
        copy.start()
        started.append(copy)
        return copy

    def local(src, dst, sem):
        copy = pltpu.make_async_copy(src, dst, sem)
        copy.start()
        return copy

    zz = block(z)
    rows_w = pl.ds(pl.multiple_of(tp * 32, 32), 32)
    there = 1 - core

    def tokens(xp, c):
        return pl.ds(pl.multiple_of((c * NX + xp) * TOK, TOK), TOK)

    partners = [device(dx=k, other=o) for k in range(1, NX) for o in (False, True)]
    partners += [device(dy=k, other=o) for k in range(1, NY) for o in (False, True)] + [device(other=True)]
    partners += [device(dz=k) for k in GREET]
    barrier = pltpu.get_barrier_semaphore()
    for partner in partners:
        pl.semaphore_signal(barrier, inc=1, device_id=partner, device_id_type=MESH)
    own_q = [local(queries, qs, loc.at[0]), local(key_cache, kc, loc.at[1]), local(value_cache, vc, loc.at[2])]
    staged = [
        local(src.at[:, y * 256 : y * 256 + 256], w_stage.at[y, b], loc.at[3 + y * 2 + b])
        for y in range(NY)
        for b, src in enumerate((w_key, w_value))
    ]
    staged += [
        local(
            hidden.at[:, b * 1024 + xp * 256 : b * 1024 + xp * 256 + 256],
            h_stage.at[xp, :, b * 256 : b * 256 + 256],
            loc.at[11 + xp * 2 + b],
        )
        for xp in range(NX)
        for b in range(2)
    ]
    pl.semaphore_wait(barrier, len(partners))
    for copy in staged:
        copy.wait()

    w1 = {}

    def wsend(k, o):
        w1[k, o] = send(
            w_stage.at[(tp + k) % NY, there if o else core], weights.at[zz, core, rows_w, :],
            w1s.at[k, o], w1r.at[k, o], device(dy=k, other=o == 1),
        )

    up, down = {}, {}

    def piece(d, k):
        rows = pl.ds(pl.multiple_of(((tp - k + NY) % NY) * 32, 32), 32)
        return weights.at[block(at_z(d)), :, rows, :]

    def zsend(k, dist, hop=1):
        if dist < 4 or k < 2:
            ref = piece(hop - dist, k)
            up[k, dist] = [send(ref, ref, zus.at[k, dist - 1], zur.at[k, dist - 1], device(dz=hop))]
        if dist < 4 or k >= 2:
            ref = piece(dist - hop, k)
            down[k, dist] = [send(ref, ref, zds.at[k, dist - 1], zdr.at[k, dist - 1], device(dz=-hop))]

    def zfirst(k):
        for dist in FIRST[k]:
            zsend(k, dist, dist)

    def zpass(k, dist):
        for copy in up.get((k, dist), []) + down.get((k, dist), []):
            copy.wait_recv()
        for hop in ONWARD[k].get(dist, ()):
            zsend(k, dist + hop, hop)

    h1 = {}

    def hsend(k):
        h1[k] = send(
            h_stage.at[(x + k) % NX], acts.at[tp, tokens(x, core), :], h1s.at[k - 1], h1r.at[k - 1], device(dx=k)
        )

    hup, hdn, hfu, hfd, hx = {}, {}, {}, {}, {}

    def chunk(dy, k):
        return acts.at[(tp + dy + NY) % NY, tokens((x - k + NX) % NX, core), :]

    def hcore(dy, k):
        ref = chunk(dy, k)
        hx[dy, k] = send(ref, ref, hxs.at[dy % NY, k], hxr.at[dy % NY, k], device(other=True))

    def ysend(k):
        ref = chunk(0, k)
        hup[k] = send(ref, ref, ups.at[k], upr.at[k], device(dy=1))
        hdn[k] = send(ref, ref, dns.at[k], dnr.at[k], device(dy=-1))
        hcore(0, k)

    def yforward(k):
        if k % 2 == 0:
            hup[k].wait_recv()
            ref = chunk(-1, k)
            hfu[k] = send(ref, ref, fus.at[k // 2], fur.at[k // 2], device(dy=1))
            hcore(-1, k)
        else:
            hdn[k].wait_recv()
            ref = chunk(1, k)
            hfd[k] = send(ref, ref, fds.at[k // 2], fdr.at[k // 2], device(dy=-1))
            hcore(1, k)

    def yother(k):
        if k % 2 == 0:
            hdn[k].wait_recv()
            hcore(1, k)
        else:
            hup[k].wait_recv()
            hcore(-1, k)

    def ylast(k):
        (hfu if k % 2 == 0 else hfd)[k].wait_recv()
        hcore(2, k)

    for k in (2, 1, 3, 0):
        for o in range(2):
            if k or o:
                wsend(k, o)
    own = [local(w_stage.at[tp, core], weights.at[zz, core, rows_w, :], loc.at[19])]
    own += [local(h_stage.at[x], acts.at[tp, tokens(x, core), :], loc.at[20])]
    for k in (2, 1, 3):
        hsend(k)
    own[1].wait()
    ysend(0)
    own[0].wait()
    w1[0, 1].wait_recv()
    zfirst(0)

    scale = HEAD ** (-0.5) * LOG2E

    def over_cache(n, kv):
        q = jnp.concatenate(
            [qs[n * STEPS : (n + 1) * STEPS, (kv * GROUP + g) * HEAD : (kv * GROUP + g + 1) * HEAD] for g in range(GROUP)],
            axis=0,
        )
        rows = slice(n * 128, (n + 1) * 128)
        qrows[kv, rows, :] = q
        keys = kc[n * CTX : (n + 1) * CTX, kv * HEAD : (kv + 1) * HEAD]
        vals = vc[n * CTX : (n + 1) * CTX, kv * HEAD : (kv + 1) * HEAD]
        score = lax.dot_general(q, keys, (((1,), (1,)), ((), ())), preferred_element_type=jnp.float32)
        live = lax.broadcasted_iota(jnp.int32, (128, CTX), 1) < lens[n]
        score = jnp.where(live, score * scale, NEG)
        top = jnp.max(score, axis=1, keepdims=True)
        e = jnp.exp2(score - top)
        total = jnp.sum(e, axis=1, keepdims=True)
        oc[kv, rows, :] = jnp.dot(e.astype(jnp.bfloat16), vals, preferred_element_type=jnp.float32)
        mc[kv, rows, :] = jnp.broadcast_to(top, (128, HEAD))
        lc[kv, rows, :] = jnp.broadcast_to(total, (128, HEAD))

    row = lax.broadcasted_iota(jnp.int32, (256, 256), 0)
    pick[...] = jnp.where(row == slots[...], 1.0, 0.0).astype(jnp.bfloat16)

    for copy in own_q:
        copy.wait()
    over_cache(0, 0)

    def wfirst(k):
        for o in range(2):
            w1[k, o].wait_recv()
        zfirst(k)

    def hfirst(k):
        h1[k].wait_recv()
        ysend(k)

    over_cache(0, 1)
    wfirst(1)
    wfirst(3)
    zpass(0, 1)
    wfirst(2)
    hfirst(1)
    hfirst(3)
    yforward(0)
    hfirst(2)
    zpass(1, 1)
    zpass(3, 1)
    yother(0)
    zpass(0, 2)
    zpass(2, 1)
    yforward(1)
    yforward(3)
    yforward(2)
    zpass(1, 2)
    zpass(3, 2)
    for k in (1, 3, 2):
        yother(k)
    zpass(0, 3)
    zpass(2, 2)
    for k in (0, 1, 3, 2):
        ylast(k)
    zpass(0, 4)
    for k in (1, 3, 2):
        zpass(k, 3)
        zpass(k, 4)
    for copy in hx.values():
        copy.wait_recv()

    total = None
    for y in range(NY):
        term = jnp.dot(
            acts[y], weights[2 * y : 2 * y + 2].reshape(512, 256), preferred_element_type=jnp.float32
        )
        total = term if total is None else total + term
    part[...] = total.reshape(2, NX, TOK, 256)
    part_send[...] = total.reshape(2, NX, TOK, 256).astype(jnp.bfloat16)
    sums = [
        send(
            part_send.at[there if o else core, (x + k) % NX], part_recv.at[o, k],
            rs.at[o, k], rr.at[o, k], device(dx=k, other=o == 1),
        )
        for k in (2, 1, 3, 0)
        for o in range(2)
        if k or o
    ]
    over_cache(1, 0)
    over_cache(1, 1)
    over_cache(2, 0)
    over_cache(2, 1)
    over_cache(3, 0)
    over_cache(3, 1)
    for copy in sums:
        copy.wait_recv()
    same, cross = part[core, x], part_recv[1, 0].astype(jnp.float32)
    for k in range(1, NX):
        same = same + part_recv[0, k].astype(jnp.float32)
        cross = cross + part_recv[1, k].astype(jnp.float32)
    fresh[core] = same.astype(jnp.bfloat16)
    fresh[there] = cross.astype(jnp.bfloat16)

    r = lax.broadcasted_iota(jnp.int32, (512, TOK), 0)
    j = lax.broadcasted_iota(jnp.int32, (512, TOK), 1)
    seen = (r // 128 == j // STEPS) & (j % STEPS <= r % STEPS)
    step = lax.broadcasted_iota(jnp.int32, (128, HEAD), 0) % STEPS
    for kv in range(2):
        keys = fresh[0, :, kv * HEAD : (kv + 1) * HEAD]
        vals = fresh[1, :, kv * HEAD : (kv + 1) * HEAD]
        score = lax.dot_general(qrows[kv], keys, (((1,), (1,)), ((), ())), preferred_element_type=jnp.float32)
        score = jnp.where(seen, score * scale, NEG)
        old = mc[kv]
        top = jnp.maximum(old, jnp.broadcast_to(jnp.max(score, axis=1, keepdims=True), (512, HEAD)))
        e = jnp.exp2(score - top[:, :TOK])
        shrink = jnp.exp2(old - top)
        denom = lc[kv] * shrink + jnp.broadcast_to(jnp.sum(e, axis=1, keepdims=True), (512, HEAD))
        value = oc[kv] * shrink + jnp.dot(e.astype(jnp.bfloat16), vals, preferred_element_type=jnp.float32)
        value = value / denom
        for n in range(SEQ):
            oc[kv, n * 128 : (n + 1) * 128, :] = jnp.where(step < rolls[n], value[n * 128 : (n + 1) * 128], 0.0)
        for q in range(32):
            send_a[kv * 32 + q] = oc[kv, pl.ds(q, 16, stride=32), :].astype(jnp.bfloat16)

    def spread(src, dst, s_sem, r_sem):
        for dx in (2, 1, 3, 0):
            for dz in (4, 3, 5, 2, 6, 1, 7, 0):
                for o in (False, True):
                    if dz or dx or o:
                        to = device(dx=dx, dz=dz, other=o)
                        pltpu.make_async_remote_copy(
                            src_ref=src.at[to[0] * 32 + to[1]], dst_ref=dst.at[me], send_sem=s_sem, recv_sem=r_sem,
                            device_id=to, device_id_type=MESH,
                        ).start()
        dst[me] = src[me]

    def arrived(buf, sem):
        some = buf.at[pl.ds(0, HOLDERS - 1)]
        pltpu.make_async_copy(some, some, sem).wait()

    spread(send_a, recv_a, a_s, a_r)
    arrived(recv_a, a_r)
    wide_a[...] = recv_a[...].reshape(1024, HEAD).astype(jnp.float32)
    for u in range(4):
        pieces = wide_a[pl.ds(u, 256, stride=4), :].astype(jnp.bfloat16)
        wide_b[pl.ds(u, 256, stride=4), :] = jnp.dot(pick[...], pieces, preferred_element_type=jnp.float32)
    send_b[...] = wide_b[...].astype(jnp.bfloat16).reshape(HOLDERS, 16, HEAD)
    spread(send_b, recv_b, b_s, b_r)
    arrived(recv_b, b_r)
    wide_a[...] = recv_b[...].reshape(1024, HEAD).astype(jnp.float32)
    for kv in range(2):
        for qh in range(2):
            for u in range(4):
                col = (kv * GROUP + 2 * u + qh) * HEAD
                for n in range(SEQ):
                    base = (kv * 2 + qh) * 256 + n * 4 + u
                    out[n * STEPS : (n + 1) * STEPS, col : col + HEAD] = wide_a[
                        pl.ds(base, 16, stride=16), :
                    ].astype(jnp.bfloat16)
    for copy in started:
        copy.wait_send()
    arrived(send_a, a_s)
    arrived(send_b, b_s)


def shards(
    w_key, w_value, hidden, queries, key_cache, value_cache, prompt_lengths, rollout_lengths, batch_slots
):
    bf, f32 = jnp.bfloat16, jnp.float32
    vm, dma = pltpu.VMEM, pltpu.SemaphoreType.DMA
    hbm = pl.BlockSpec(memory_space=pl.ANY)
    smem = pl.BlockSpec(memory_space=pltpu.SMEM)
    vmem = pl.BlockSpec(memory_space=pltpu.VMEM)
    scratch = [
        vm((NY, 2, 32, 256), bf),
        vm((NX, TOK, 512), bf),
        vm((NY, 2 * NX * TOK, 512), bf),
        vm((NZ, 2, 128, 256), bf),
        vm((TOK, 2048), bf),
        vm((SEQ * CTX, 256), bf),
        vm((SEQ * CTX, 256), bf),
        vm((2, NX, TOK, 256), f32),
        vm((2, NX, TOK, 256), bf),
        vm((2, NX, TOK, 256), bf),
        vm((2, TOK, 256), bf),
        vm((2, 512, HEAD), bf),
        vm((2, 512, HEAD), f32),
        vm((2, 512, HEAD), f32),
        vm((2, 512, HEAD), f32),
        vm((256, 256), bf),
    ]
    scratch += [vm((HOLDERS, 16, HEAD), bf)] * 4 + [vm((1024, HEAD), f32)] * 2
    scratch += [dma((21,))]
    scratch += [dma((4, 2))] * 2 + [dma((3,))] * 2
    scratch += [dma((4,))] * 4 + [dma((2,))] * 4 + [dma((4, 4))] * 2
    scratch += [dma((4, 4))] * 4
    scratch += [dma((2, 4))] * 2
    scratch += [dma] * 4
    result = pl.pallas_call(
        kernel,
        out_shape=jax.ShapeDtypeStruct((TOK, 2048), bf),
        in_specs=[smem, smem, vmem] + [hbm] * 6,
        out_specs=vmem,
        scratch_shapes=scratch,
        compiler_params=pltpu.CompilerParams(collective_id=0, has_side_effects=True, vmem_limit_bytes=60 * 1024 * 1024),
        name="rollout",
    )(
        prompt_lengths,
        rollout_lengths,
        batch_slots.reshape(1, 256),
        w_key,
        w_value,
        hidden.reshape(TOK, 2048),
        queries.reshape(TOK, 2048),
        key_cache.reshape(SEQ * CTX, 256),
        value_cache.reshape(SEQ * CTX, 256),
    )
    return result.reshape(SEQ, STEPS, 2048)


def solution(mesh):
    rows = P(("sect", "dp", "tp"), None)
    spread = P(("sect", "dp"), None, "tp")
    each = P(("sect", "dp"))
    return jax.shard_map(
        shards,
        mesh=mesh,
        in_specs=(rows, rows, spread, spread, spread, spread, each, each, P()),
        out_specs=spread,
        check_vma=False,
    )
```

```python
import functools

import jax
import jax.numpy as jnp
from jax import lax
from jax.experimental import pallas as pl
from jax.experimental.pallas import tpu as pltpu
from jax.sharding import PartitionSpec as P

MESH = pl.DeviceIdType.MESH
HEAD = 128
STEPS = 16
CTX = 512
GROUP = 8
SEQ = 4
TOK = SEQ * STEPS
NX, NY, NZ = 4, 4, 8
HOLDERS = 64
LOG2E = 1.4426950408889634
NEG = -1e30
FIRST = [(1,), (1,), (1,), (1,)]
ONWARD = [{1: (1,), 2: (1, 2)}] * 4
GREET = (-1, 1)
STRAIGHT = ()


def kernel(
    lens, rolls, slots, w_key, w_value, hidden, queries, key_cache, value_cache, out,
    w_stage, h_stage, acts, weights, qs, kc, vc, part, part_send, part_recv, fresh, qrows, oc, mc, lc, pick,
    send_a, recv_a, send_b, recv_b, wide_a, wide_b, send_c, recv_c, recv_d, send_d, small, old,
    loc, w1s, w1r, h1s, h1r, ups, upr, dns, dnr, hfs, hfr, hxs, hxr,
    zus, zur, zds, zdr, rs, rr, a_s, a_r, b_s, b_r, c_s, c_r, d_s, d_r,
):
    sect, dp, tp = lax.axis_index("sect"), lax.axis_index("dp"), lax.axis_index("tp")
    z_hi, x, core = dp // 8, (dp // 2) % 4, dp % 2
    z = 2 * z_hi + sect
    me = sect * 32 + dp

    def at_z(d):
        return (z + d + NZ) % NZ

    def block(zp):
        return (zp % 2) * 4 + zp // 2

    def device(dx=0, dy=0, dz=0, other=False):
        zp = at_z(dz)
        c = 1 - core if other else core
        return (zp % 2, (zp // 2) * 8 + ((x + dx + NX) % NX) * 2 + c, (tp + dy + NY) % NY)

    started = []

    def send(src, dst, s_sem, r_sem, to):
        copy = pltpu.make_async_remote_copy(
            src_ref=src, dst_ref=dst, send_sem=s_sem, recv_sem=r_sem, device_id=to, device_id_type=MESH
        )
        copy.start()
        started.append(copy)
        return copy

    def local(src, dst, sem):
        copy = pltpu.make_async_copy(src, dst, sem)
        copy.start()
        return copy

    zz = block(z)
    rows_w = pl.ds(pl.multiple_of(tp * 32, 32), 32)
    there = 1 - core

    def tokens(xp, c):
        return pl.ds(pl.multiple_of((c * NX + xp) * TOK, TOK), TOK)

    partners = [device(dx=k, other=o) for k in range(1, NX) for o in (False, True)]
    partners += [device(dy=k, other=o) for k in range(1, NY) for o in (False, True)] + [device(other=True)]
    partners += [device(dz=k) for k in GREET]
    barrier = pltpu.get_barrier_semaphore()
    for partner in partners:
        pl.semaphore_signal(barrier, inc=1, device_id=partner, device_id_type=MESH)
    own_q = [local(queries, qs, loc.at[0]), local(key_cache, kc, loc.at[1]), local(value_cache, vc, loc.at[2])]
    staged = [
        local(src.at[:, y * 256 : y * 256 + 256], w_stage.at[y, b], loc.at[3 + y * 2 + b])
        for y in range(NY)
        for b, src in enumerate((w_key, w_value))
    ]
    staged += [
        local(
            hidden.at[:, b * 1024 + xp * 256 : b * 1024 + xp * 256 + 256],
            h_stage.at[xp, :, b * 256 : b * 256 + 256],
            loc.at[11 + xp * 2 + b],
        )
        for xp in range(NX)
        for b in range(2)
    ]
    pl.semaphore_wait(barrier, len(partners))
    for copy in staged:
        copy.wait()

    w1 = {}

    def wsend(k, o):
        w1[k, o] = send(
            w_stage.at[(tp + k) % NY, there if o else core], weights.at[zz, core, rows_w, :],
            w1s.at[k, o], w1r.at[k, o], device(dy=k, other=o == 1),
        )

    up, down = {}, {}

    def piece(d, k):
        rows = pl.ds(pl.multiple_of(((tp - k + NY) % NY) * 32, 32), 32)
        return weights.at[block(at_z(d)), :, rows, :]

    def zsend(k, dist, hop=1):
        if dist < 4 or k < 2:
            ref = piece(hop - dist, k)
            up[k, dist] = [send(ref, ref, zus.at[k, dist - 1], zur.at[k, dist - 1], device(dz=hop))]
        if dist < 4 or k >= 2:
            ref = piece(dist - hop, k)
            down[k, dist] = [send(ref, ref, zds.at[k, dist - 1], zdr.at[k, dist - 1], device(dz=-hop))]

    def zfirst(k):
        for dist in FIRST[k]:
            zsend(k, dist, dist)

    def zpass(k, dist):
        for copy in up.get((k, dist), []) + down.get((k, dist), []):
            copy.wait_recv()
        for hop in ONWARD[k].get(dist, ()):
            zsend(k, dist + hop, hop)

    h1 = {}

    def hsend(k):
        h1[k] = send(
            h_stage.at[(x + k) % NX], acts.at[tp, tokens(x, core), :], h1s.at[k - 1], h1r.at[k - 1], device(dx=k)
        )

    hup, hdn, hfar, hx = {}, {}, {}, {}

    def chunk(dy, k):
        return acts.at[(tp + dy + NY) % NY, tokens((x - k + NX) % NX, core), :]

    def hcore(dy, k):
        ref = chunk(dy, k)
        hx[dy, k] = send(ref, ref, hxs.at[dy % NY, k], hxr.at[dy % NY, k], device(other=True))

    def ysend(k):
        ref = chunk(0, k)
        hup[k] = send(ref, ref, ups.at[k], upr.at[k], device(dy=1))
        hdn[k] = send(ref, ref, dns.at[k], dnr.at[k], device(dy=-1))
        if k in STRAIGHT:
            hfar[k] = send(ref, ref, hfs.at[k], hfr.at[k], device(dy=2))
        hcore(0, k)

    def yforward(k):
        if k % 2 == 0:
            hup[k].wait_recv()
            ref = chunk(-1, k)
            if k not in STRAIGHT:
                hfar[k] = send(ref, ref, hfs.at[k], hfr.at[k], device(dy=1))
            hcore(-1, k)
        else:
            hdn[k].wait_recv()
            ref = chunk(1, k)
            if k not in STRAIGHT:
                hfar[k] = send(ref, ref, hfs.at[k], hfr.at[k], device(dy=-1))
            hcore(1, k)

    def yother(k):
        if k % 2 == 0:
            hdn[k].wait_recv()
            hcore(1, k)
        else:
            hup[k].wait_recv()
            hcore(-1, k)

    def ylast(k):
        hfar[k].wait_recv()
        hcore(2, k)

    for k in (2, 1, 3, 0):
        for o in range(2):
            if k or o:
                wsend(k, o)
    own = [local(w_stage.at[tp, core], weights.at[zz, core, rows_w, :], loc.at[19])]
    own += [local(h_stage.at[x], acts.at[tp, tokens(x, core), :], loc.at[20])]
    for k in (2, 1, 3):
        hsend(k)
    own[1].wait()
    ysend(0)
    own[0].wait()
    w1[0, 1].wait_recv()
    zfirst(0)

    scale = HEAD ** (-0.5) * LOG2E

    def over_cache(n, kv):
        q = jnp.concatenate(
            [qs[n * STEPS : (n + 1) * STEPS, (kv * GROUP + g) * HEAD : (kv * GROUP + g + 1) * HEAD] for g in range(GROUP)],
            axis=0,
        )
        rows = slice(n * 128, (n + 1) * 128)
        qrows[kv, rows, :] = q
        keys = kc[n * CTX : (n + 1) * CTX, kv * HEAD : (kv + 1) * HEAD]
        vals = vc[n * CTX : (n + 1) * CTX, kv * HEAD : (kv + 1) * HEAD]
        score = lax.dot_general(q, keys, (((1,), (1,)), ((), ())), preferred_element_type=jnp.float32)
        live = lax.broadcasted_iota(jnp.int32, (128, CTX), 1) < lens[n]
        score = jnp.where(live, score * scale, NEG)
        top = jnp.max(score, axis=1, keepdims=True)
        e = jnp.exp2(score - top)
        total = jnp.sum(e, axis=1, keepdims=True)
        value = jnp.dot(e.astype(jnp.bfloat16), vals, preferred_element_type=jnp.float32)
        oc[kv, rows, :] = value / total
        mc[kv * SEQ + n, :, :] = jnp.transpose(jnp.broadcast_to(top, (128, HEAD)))[:8]
        lc[kv * SEQ + n, :, :] = jnp.transpose(jnp.broadcast_to(total, (128, HEAD)))[:8]

    def spread(src, dst, s_sem, r_sem):
        for dx in (2, 1, 3, 0):
            for dz in (4, 3, 5, 2, 6, 1, 7, 0):
                for o in (False, True):
                    if dz or dx or o:
                        to = device(dx=dx, dz=dz, other=o)
                        pltpu.make_async_remote_copy(
                            src_ref=src.at[to[0] * 32 + to[1]], dst_ref=dst.at[me], send_sem=s_sem, recv_sem=r_sem,
                            device_id=to, device_id_type=MESH,
                        ).start()
        dst[me] = src[me]

    def arrived(buf, sem):
        some = buf.at[pl.ds(0, HOLDERS - 1)]
        pltpu.make_async_copy(some, some, sem).wait()

    row = lax.broadcasted_iota(jnp.int32, (256, 256), 0)
    pick[...] = jnp.where(row == slots[...], 1.0, 0.0).astype(jnp.bfloat16)

    for copy in own_q:
        copy.wait()
    over_cache(0, 0)

    def wfirst(k):
        for o in range(2):
            w1[k, o].wait_recv()
        zfirst(k)

    def hfirst(k):
        h1[k].wait_recv()
        ysend(k)

    def tiles(kv):
        for q in range(32):
            send_a[kv * 32 + q] = oc[kv, pl.ds(q, 16, stride=32), :].astype(jnp.bfloat16)

    wfirst(1)
    wfirst(3)
    zpass(0, 1)
    wfirst(2)
    hfirst(1)
    hfirst(3)
    yforward(0)
    hfirst(2)
    over_cache(1, 0)
    over_cache(2, 0)
    zpass(1, 1)
    zpass(3, 1)
    yother(0)
    zpass(0, 2)
    zpass(2, 1)
    yforward(1)
    yforward(3)
    yforward(2)
    over_cache(3, 0)
    tiles(0)
    over_cache(0, 1)
    over_cache(1, 1)
    zpass(1, 2)
    zpass(3, 2)
    for k in (1, 3, 2):
        yother(k)
    zpass(0, 3)
    zpass(2, 2)
    over_cache(2, 1)
    over_cache(3, 1)
    tiles(1)
    for k in (0, 1, 3, 2):
        ylast(k)
    zpass(0, 4)
    for k in (1, 3, 2):
        zpass(k, 3)
    for k in (1, 3, 2):
        zpass(k, 4)
    for copy in hx.values():
        copy.wait_recv()

    spread(send_a, recv_a, a_s, a_r)
    total = None
    for y in range(NY):
        term = jnp.dot(
            acts[y], weights[2 * y : 2 * y + 2].reshape(512, 256), preferred_element_type=jnp.float32
        )
        total = term if total is None else total + term
    part[...] = total.reshape(2, NX, TOK, 256)
    part_send[...] = total.reshape(2, NX, TOK, 256).astype(jnp.bfloat16)
    sums = [
        send(
            part_send.at[there if o else core, (x + k) % NX], part_recv.at[o, k],
            rs.at[o, k], rr.at[o, k], device(dx=k, other=o == 1),
        )
        for k in (2, 1, 3, 0)
        for o in range(2)
        if k or o
    ]
    for copy in sums:
        copy.wait_recv()
    same, cross = part[core, x], part_recv[1, 0].astype(jnp.float32)
    for k in range(1, NX):
        same = same + part_recv[0, k].astype(jnp.float32)
        cross = cross + part_recv[1, k].astype(jnp.float32)
    fresh[core] = same.astype(jnp.bfloat16)
    fresh[there] = cross.astype(jnp.bfloat16)

    r = lax.broadcasted_iota(jnp.int32, (STEPS, 128), 1) % STEPS
    seen = lax.broadcasted_iota(jnp.int32, (STEPS, 128), 0) <= r
    small[16 * 16 :, :] = jnp.zeros((16, HEAD), jnp.float32)
    for kv in range(2):
        for n in range(SEQ):
            keys = fresh[0, n * STEPS : (n + 1) * STEPS, kv * HEAD : (kv + 1) * HEAD]
            score = lax.dot_general(
                keys, qrows[kv, n * 128 : (n + 1) * 128, :], (((1,), (1,)), ((), ())),
                preferred_element_type=jnp.float32,
            )
            score = jnp.where(seen, score * scale, NEG)
            before = mc[kv * SEQ + n, 0:1, :]
            top = jnp.maximum(before, jnp.max(score, axis=0, keepdims=True))
            e = jnp.exp2(score - top)
            cached = lc[kv * SEQ + n, 0:1, :] * jnp.exp2(before - top)
            factor = 1.0 / (cached + jnp.sum(e, axis=0, keepdims=True))
            factor = jnp.where(r[0:1, :] < rolls[n], factor, 0.0)
            small[pl.ds(kv * TOK + n * STEPS, STEPS), :] = e * factor
            small[pl.ds(16 * 16 + n * 4 + kv, 1), :] = cached * factor
        small[pl.ds((2 + kv) * TOK, TOK), :] = fresh[1, :, kv * HEAD : (kv + 1) * HEAD].astype(jnp.float32)
    for part_ in range(4):
        for jq in range(4):
            send_c[part_ * 4 + jq] = small[pl.ds(part_ * TOK + jq, 16, stride=4), :].astype(jnp.bfloat16)
    send_c[16] = small[pl.ds(16 * 16, 16), :].astype(jnp.bfloat16)

    def middle(t):
        zp = t // 2 if t < 16 else 0
        xp = (t % 2) * 2 + zp % 2 if t < 16 else 1
        c = 0 if t < 16 else 1
        return zp % 2, (zp // 2) * 8 + xp * 2 + c

    places = [middle(t) for t in range(17)]
    middles = [a * 32 + b for a, b in places]
    mine = functools.reduce(jnp.logical_or, [me == m for m in middles])
    for t in sorted(range(17), key=lambda t: -t):
        @pl.when(me != middles[t])
        def _(t=t):
            pltpu.make_async_remote_copy(
                src_ref=send_c.at[t], dst_ref=recv_c.at[me], send_sem=c_s, recv_sem=c_r,
                device_id=(*places[t], tp), device_id_type=MESH,
            ).start()

        @pl.when(me == middles[t])
        def _(t=t):
            recv_c[me] = send_c[t]

    def wait_tiles(buf, sem, count):
        some = buf.at[pl.ds(0, count)]
        pltpu.make_async_copy(some, some, sem).wait()

    def reorder(src, dst):
        wide_a[...] = src[...].reshape(1024, HEAD).astype(jnp.float32)
        for u in range(4):
            pieces = wide_a[pl.ds(u, 256, stride=4), :].astype(jnp.bfloat16)
            wide_b[pl.ds(u, 256, stride=4), :] = jnp.dot(pick[...], pieces, preferred_element_type=jnp.float32)
        dst[...] = wide_b[...].astype(jnp.bfloat16).reshape(HOLDERS, 16, HEAD)

    arrived(recv_a, a_r)
    reorder(recv_a, send_b)
    spread(send_b, recv_b, b_s, b_r)

    @pl.when(mine)
    def _():
        wait_tiles(recv_c, c_r, HOLDERS - 1)
        reorder(recv_c, send_d)
        tile = jnp.where(core == 1, 16, 2 * z + x // 2)
        for dx in (2, 1, 3, 0):
            for dz in (4, 3, 5, 2, 6, 1, 7, 0):
                for o in (False, True):
                    if dz or dx or o:
                        to = device(dx=dx, dz=dz, other=o)
                        pltpu.make_async_remote_copy(
                            src_ref=send_d.at[to[0] * 32 + to[1]], dst_ref=recv_d.at[tile], send_sem=d_s, recv_sem=d_r,
                            device_id=to, device_id_type=MESH,
                        ).start()
        recv_d[tile] = send_d[me]

    arrived(recv_b, b_r)
    wide_a[...] = recv_b[...].reshape(1024, HEAD).astype(jnp.float32)
    for kv in range(2):
        for n in range(SEQ):
            for g in range(GROUP):
                old[kv, n, g * STEPS : (g + 1) * STEPS, :] = wide_a[
                    pl.ds((kv * 2 + g % 2) * 256 + n * 4 + g // 2, 16, stride=16), :
                ].astype(jnp.bfloat16)

    @pl.when(mine)
    def _():
        wait_tiles(recv_d, d_r, 16)
        wait_tiles(send_c, c_s, 16)
        wait_tiles(send_d, d_s, HOLDERS - 1)

    @pl.when(jnp.logical_not(mine))
    def _():
        wait_tiles(recv_d, d_r, 17)
        wait_tiles(send_c, c_s, 17)

    small[...] = recv_d[...].reshape(17 * 16, HEAD).astype(jnp.float32)
    owner = (lax.broadcasted_iota(jnp.int32, (TOK, HEAD), 0) // 4) % 4
    eye = lax.broadcasted_iota(jnp.int32, (128, 128), 0) == lax.broadcasted_iota(jnp.int32, (128, 128), 1)
    for kv in range(2):
        new_w = small[pl.ds(kv * TOK, TOK), :]
        new_v = small[pl.ds((2 + kv) * TOK, TOK), :].astype(jnp.bfloat16)
        for n in range(SEQ):
            share = jnp.broadcast_to(small[pl.ds(16 * 16 + n * 4 + kv, 1), :], (128, 128))
            value = jnp.dot(jnp.where(eye, share, 0.0).astype(jnp.bfloat16), old[kv, n], preferred_element_type=jnp.float32)
            value += lax.dot_general(
                jnp.where(owner == n, new_w, 0.0).astype(jnp.bfloat16), new_v, (((0,), (0,)), ((), ())),
                preferred_element_type=jnp.float32,
            )
            value = value.astype(jnp.bfloat16)
            for g in range(GROUP):
                col = (kv * GROUP + g) * HEAD
                out[n * STEPS : (n + 1) * STEPS, col : col + HEAD] = value[g * STEPS : (g + 1) * STEPS]
    for copy in started:
        copy.wait_send()
    arrived(send_a, a_s)
    arrived(send_b, b_s)


def shards(
    w_key, w_value, hidden, queries, key_cache, value_cache, prompt_lengths, rollout_lengths, batch_slots
):
    bf, f32 = jnp.bfloat16, jnp.float32
    vm, dma = pltpu.VMEM, pltpu.SemaphoreType.DMA
    hbm = pl.BlockSpec(memory_space=pl.ANY)
    smem = pl.BlockSpec(memory_space=pltpu.SMEM)
    vmem = pl.BlockSpec(memory_space=pltpu.VMEM)
    scratch = [
        vm((NY, 2, 32, 256), bf),
        vm((NX, TOK, 512), bf),
        vm((NY, 2 * NX * TOK, 512), bf),
        vm((NZ, 2, 128, 256), bf),
        vm((TOK, 2048), bf),
        vm((SEQ * CTX, 256), bf),
        vm((SEQ * CTX, 256), bf),
        vm((2, NX, TOK, 256), f32),
        vm((2, NX, TOK, 256), bf),
        vm((2, NX, TOK, 256), bf),
        vm((2, TOK, 256), bf),
        vm((2, 512, HEAD), bf),
        vm((2, 512, HEAD), f32),
        vm((2 * SEQ, 8, HEAD), f32),
        vm((2 * SEQ, 8, HEAD), f32),
        vm((256, 256), bf),
    ]
    scratch += [vm((HOLDERS, 16, HEAD), bf)] * 4 + [vm((1024, HEAD), f32)] * 2
    scratch += [vm((17, 16, HEAD), bf), vm((HOLDERS, 16, HEAD), bf)] * 2 + [vm((17 * 16, HEAD), f32), vm((2, SEQ, 128, HEAD), bf)]
    scratch += [dma((21,))]
    scratch += [dma((4, 2))] * 2 + [dma((3,))] * 2
    scratch += [dma((4,))] * 6 + [dma((4, 4))] * 2
    scratch += [dma((4, 4))] * 4
    scratch += [dma((2, 4))] * 2
    scratch += [dma] * 8
    result = pl.pallas_call(
        kernel,
        out_shape=jax.ShapeDtypeStruct((TOK, 2048), bf),
        in_specs=[smem, smem, vmem] + [hbm] * 6,
        out_specs=vmem,
        scratch_shapes=scratch,
        compiler_params=pltpu.CompilerParams(collective_id=0, has_side_effects=True, vmem_limit_bytes=60 * 1024 * 1024),
        name="rollout",
    )(
        prompt_lengths,
        rollout_lengths,
        batch_slots.reshape(1, 256),
        w_key,
        w_value,
        hidden.reshape(TOK, 2048),
        queries.reshape(TOK, 2048),
        key_cache.reshape(SEQ * CTX, 256),
        value_cache.reshape(SEQ * CTX, 256),
    )
    return result.reshape(SEQ, STEPS, 2048)


def solution(mesh):
    rows = P(("sect", "dp", "tp"), None)
    spread = P(("sect", "dp"), None, "tp")
    each = P(("sect", "dp"))
    return jax.shard_map(
        shards,
        mesh=mesh,
        in_specs=(rows, rows, spread, spread, spread, spread, each, each, P()),
        out_specs=spread,
        check_vma=False,
    )
```

```python
import functools

import jax
import jax.numpy as jnp
from jax import lax
from jax.experimental import pallas as pl
from jax.experimental.pallas import tpu as pltpu
from jax.sharding import PartitionSpec as P

MESH = pl.DeviceIdType.MESH
HEAD = 128
STEPS = 16
CTX = 512
GROUP = 8
SEQ = 4
TOK = SEQ * STEPS
NX, NY, NZ = 4, 4, 8
HOLDERS = 64
LOG2E = 1.4426950408889634
NEG = -1e30
FIRST = [(1,), (1,), (1,), (1,)]
ONWARD = [{1: (1,), 2: (1, 2)}] * 4
GREET = (-1, 1)
STRAIGHT = ()


def kernel(
    lens, rolls, slots, w_key, w_value, hidden, queries, key_cache, value_cache, out,
    w_stage, h_stage, acts, weights, qs, kc, vc, part, part_send, part_recv, fresh, qrows, oc, mc, lc, pick,
    send_a, recv_a, send_b, recv_b, wide_a, wide_b, send_c, recv_c, recv_d, send_d, small, old,
    loc, w1s, w1r, h1s, h1r, ups, upr, dns, dnr, hfs, hfr, hxs, hxr,
    zus, zur, zds, zdr, rs, rr, a_s, a_r, b_s, b_r, c_s, c_r, d_s, d_r,
):
    sect, dp, tp = lax.axis_index("sect"), lax.axis_index("dp"), lax.axis_index("tp")
    z_hi, x, core = dp // 8, (dp // 2) % 4, dp % 2
    z = 2 * z_hi + sect
    me = sect * 32 + dp

    def at_z(d):
        return (z + d + NZ) % NZ

    def block(zp):
        return (zp % 2) * 4 + zp // 2

    def device(dx=0, dy=0, dz=0, other=False):
        zp = at_z(dz)
        c = 1 - core if other else core
        return (zp % 2, (zp // 2) * 8 + ((x + dx + NX) % NX) * 2 + c, (tp + dy + NY) % NY)

    started = []

    def send(src, dst, s_sem, r_sem, to):
        copy = pltpu.make_async_remote_copy(
            src_ref=src, dst_ref=dst, send_sem=s_sem, recv_sem=r_sem, device_id=to, device_id_type=MESH
        )
        copy.start()
        started.append(copy)
        return copy

    def local(src, dst, sem):
        copy = pltpu.make_async_copy(src, dst, sem)
        copy.start()
        return copy

    zz = block(z)
    rows_w = pl.ds(pl.multiple_of(tp * 32, 32), 32)
    there = 1 - core

    def tokens(xp, c):
        return pl.ds(pl.multiple_of((c * NX + xp) * TOK, TOK), TOK)

    partners = [device(dx=k, other=o) for k in range(1, NX) for o in (False, True)]
    partners += [device(dy=k, other=o) for k in range(1, NY) for o in (False, True)] + [device(other=True)]
    partners += [device(dz=k) for k in GREET]
    barrier = pltpu.get_barrier_semaphore()
    for partner in partners:
        pl.semaphore_signal(barrier, inc=1, device_id=partner, device_id_type=MESH)
    own_q = [local(queries, qs, loc.at[0]), local(key_cache, kc, loc.at[1]), local(value_cache, vc, loc.at[2])]
    staged = [
        local(src.at[:, y * 256 : y * 256 + 256], w_stage.at[y, b], loc.at[3 + y * 2 + b])
        for y in range(NY)
        for b, src in enumerate((w_key, w_value))
    ]
    staged += [
        local(
            hidden.at[:, b * 1024 + xp * 256 : b * 1024 + xp * 256 + 256],
            h_stage.at[xp, :, b * 256 : b * 256 + 256],
            loc.at[11 + xp * 2 + b],
        )
        for xp in range(NX)
        for b in range(2)
    ]
    pl.semaphore_wait(barrier, len(partners))
    for copy in staged:
        copy.wait()

    w1 = {}

    def wsend(k, o):
        w1[k, o] = send(
            w_stage.at[(tp + k) % NY, there if o else core], weights.at[zz, core, rows_w, :],
            w1s.at[k, o], w1r.at[k, o], device(dy=k, other=o == 1),
        )

    up, down = {}, {}

    def piece(d, k):
        rows = pl.ds(pl.multiple_of(((tp - k + NY) % NY) * 32, 32), 32)
        return weights.at[block(at_z(d)), :, rows, :]

    def zsend(k, dist, hop=1):
        if dist < 4 or k < 2:
            ref = piece(hop - dist, k)
            up[k, dist] = [send(ref, ref, zus.at[k, dist - 1], zur.at[k, dist - 1], device(dz=hop))]
        if dist < 4 or k >= 2:
            ref = piece(dist - hop, k)
            down[k, dist] = [send(ref, ref, zds.at[k, dist - 1], zdr.at[k, dist - 1], device(dz=-hop))]

    def zfirst(k):
        for dist in FIRST[k]:
            zsend(k, dist, dist)

    def zpass(k, dist):
        for copy in up.get((k, dist), []) + down.get((k, dist), []):
            copy.wait_recv()
        for hop in ONWARD[k].get(dist, ()):
            zsend(k, dist + hop, hop)

    h1 = {}

    def hsend(k):
        h1[k] = send(
            h_stage.at[(x + k) % NX], acts.at[tp, tokens(x, core), :], h1s.at[k - 1], h1r.at[k - 1], device(dx=k)
        )

    hup, hdn, hfar, hx = {}, {}, {}, {}

    def chunk(dy, k):
        return acts.at[(tp + dy + NY) % NY, tokens((x - k + NX) % NX, core), :]

    def hcore(dy, k):
        ref = chunk(dy, k)
        hx[dy, k] = send(ref, ref, hxs.at[dy % NY, k], hxr.at[dy % NY, k], device(other=True))

    def ysend(k):
        ref = chunk(0, k)
        hup[k] = send(ref, ref, ups.at[k], upr.at[k], device(dy=1))
        hdn[k] = send(ref, ref, dns.at[k], dnr.at[k], device(dy=-1))
        if k in STRAIGHT:
            hfar[k] = send(ref, ref, hfs.at[k], hfr.at[k], device(dy=2))
        hcore(0, k)

    def yforward(k):
        if k % 2 == 0:
            hup[k].wait_recv()
            ref = chunk(-1, k)
            if k not in STRAIGHT:
                hfar[k] = send(ref, ref, hfs.at[k], hfr.at[k], device(dy=1))
            hcore(-1, k)
        else:
            hdn[k].wait_recv()
            ref = chunk(1, k)
            if k not in STRAIGHT:
                hfar[k] = send(ref, ref, hfs.at[k], hfr.at[k], device(dy=-1))
            hcore(1, k)

    def yother(k):
        if k % 2 == 0:
            hdn[k].wait_recv()
            hcore(1, k)
        else:
            hup[k].wait_recv()
            hcore(-1, k)

    def ylast(k):
        hfar[k].wait_recv()
        hcore(2, k)

    for k in (2, 1, 3, 0):
        for o in range(2):
            if k or o:
                wsend(k, o)
    own = [local(w_stage.at[tp, core], weights.at[zz, core, rows_w, :], loc.at[19])]
    own += [local(h_stage.at[x], acts.at[tp, tokens(x, core), :], loc.at[20])]
    for k in (2, 1, 3):
        hsend(k)
    own[1].wait()
    ysend(0)
    own[0].wait()
    w1[0, 1].wait_recv()
    zfirst(0)

    scale = HEAD ** (-0.5) * LOG2E

    def over_cache(n, kv):
        q = jnp.concatenate(
            [qs[n * STEPS : (n + 1) * STEPS, (kv * GROUP + g) * HEAD : (kv * GROUP + g + 1) * HEAD] for g in range(GROUP)],
            axis=0,
        )
        rows = slice(n * 128, (n + 1) * 128)
        qrows[kv, rows, :] = q
        keys = kc[n * CTX : (n + 1) * CTX, kv * HEAD : (kv + 1) * HEAD]
        vals = vc[n * CTX : (n + 1) * CTX, kv * HEAD : (kv + 1) * HEAD]
        score = lax.dot_general(q, keys, (((1,), (1,)), ((), ())), preferred_element_type=jnp.float32)
        live = lax.broadcasted_iota(jnp.int32, (128, CTX), 1) < lens[n]
        score = jnp.where(live, score * scale, NEG)
        top = jnp.max(score, axis=1, keepdims=True)
        e = jnp.exp2(score - top)
        total = jnp.sum(e, axis=1, keepdims=True)
        value = jnp.dot(e.astype(jnp.bfloat16), vals, preferred_element_type=jnp.float32)
        oc[kv, rows, :] = value / total
        mc[kv * SEQ + n, :, :] = jnp.transpose(jnp.broadcast_to(top, (128, HEAD)))[:8]
        lc[kv * SEQ + n, :, :] = jnp.transpose(jnp.broadcast_to(total, (128, HEAD)))[:8]

    def spread(src, dst, s_sem, r_sem, columns=(2, 1, 3, 0)):
        for dx in columns:
            for dz in (4, 3, 5, 2, 6, 1, 7, 0):
                for o in (False, True):
                    if dz or dx or o:
                        to = device(dx=dx, dz=dz, other=o)
                        pltpu.make_async_remote_copy(
                            src_ref=src.at[to[0] * 32 + to[1]], dst_ref=dst.at[me], send_sem=s_sem, recv_sem=r_sem,
                            device_id=to, device_id_type=MESH,
                        ).start()
        if 0 in columns:
            dst[me] = src[me]

    def arrived(buf, sem):
        some = buf.at[pl.ds(0, HOLDERS - 1)]
        pltpu.make_async_copy(some, some, sem).wait()

    row = lax.broadcasted_iota(jnp.int32, (256, 256), 0)
    pick[...] = jnp.where(row == slots[...], 1.0, 0.0).astype(jnp.bfloat16)

    for copy in own_q:
        copy.wait()
    over_cache(0, 0)
    over_cache(1, 0)
    over_cache(2, 0)
    over_cache(3, 0)

    def wfirst(k):
        for o in range(2):
            w1[k, o].wait_recv()
        zfirst(k)

    def hfirst(k):
        h1[k].wait_recv()
        ysend(k)

    def tiles(kv):
        for q in range(32):
            send_a[kv * 32 + q] = oc[kv, pl.ds(q, 16, stride=32), :].astype(jnp.bfloat16)

    wfirst(1)
    wfirst(3)
    zpass(0, 1)
    wfirst(2)
    hfirst(1)
    hfirst(3)
    yforward(0)
    hfirst(2)
    zpass(1, 1)
    zpass(3, 1)
    yother(0)
    zpass(0, 2)
    zpass(2, 1)
    yforward(1)
    yforward(3)
    yforward(2)
    tiles(0)
    over_cache(0, 1)
    over_cache(1, 1)
    zpass(1, 2)
    zpass(3, 2)
    for k in (1, 3, 2):
        yother(k)
    zpass(0, 3)
    zpass(2, 2)
    over_cache(2, 1)
    over_cache(3, 1)
    tiles(1)
    for k in (0, 1, 3, 2):
        ylast(k)
    zpass(0, 4)
    for k in (1, 3, 2):
        zpass(k, 3)
    for k in (1, 3, 2):
        zpass(k, 4)
    for copy in hx.values():
        copy.wait_recv()

    spread(send_a, recv_a, a_s, a_r)
    total = None
    for y in range(NY):
        term = jnp.dot(
            acts[y], weights[2 * y : 2 * y + 2].reshape(512, 256), preferred_element_type=jnp.float32
        )
        total = term if total is None else total + term
    part[...] = total.reshape(2, NX, TOK, 256)
    part_send[...] = total.reshape(2, NX, TOK, 256).astype(jnp.bfloat16)
    sums = [
        send(
            part_send.at[there if o else core, (x + k) % NX], part_recv.at[o, k],
            rs.at[o, k], rr.at[o, k], device(dx=k, other=o == 1),
        )
        for k in (2, 1, 3, 0)
        for o in range(2)
        if k or o
    ]
    for copy in sums:
        copy.wait_recv()
    same, cross = part[core, x], part_recv[1, 0].astype(jnp.float32)
    for k in range(1, NX):
        same = same + part_recv[0, k].astype(jnp.float32)
        cross = cross + part_recv[1, k].astype(jnp.float32)
    fresh[core] = same.astype(jnp.bfloat16)
    fresh[there] = cross.astype(jnp.bfloat16)

    r = lax.broadcasted_iota(jnp.int32, (STEPS, 128), 1) % STEPS
    seen = lax.broadcasted_iota(jnp.int32, (STEPS, 128), 0) <= r
    small[16 * 16 :, :] = jnp.zeros((16, HEAD), jnp.float32)
    for kv in range(2):
        for n in range(SEQ):
            keys = fresh[0, n * STEPS : (n + 1) * STEPS, kv * HEAD : (kv + 1) * HEAD]
            score = lax.dot_general(
                keys, qrows[kv, n * 128 : (n + 1) * 128, :], (((1,), (1,)), ((), ())),
                preferred_element_type=jnp.float32,
            )
            score = jnp.where(seen, score * scale, NEG)
            before = mc[kv * SEQ + n, 0:1, :]
            top = jnp.maximum(before, jnp.max(score, axis=0, keepdims=True))
            e = jnp.exp2(score - top)
            cached = lc[kv * SEQ + n, 0:1, :] * jnp.exp2(before - top)
            factor = 1.0 / (cached + jnp.sum(e, axis=0, keepdims=True))
            factor = jnp.where(r[0:1, :] < rolls[n], factor, 0.0)
            small[pl.ds(kv * TOK + n * STEPS, STEPS), :] = e * factor
            small[pl.ds(16 * 16 + n * 4 + kv, 1), :] = cached * factor
        small[pl.ds((2 + kv) * TOK, TOK), :] = fresh[1, :, kv * HEAD : (kv + 1) * HEAD].astype(jnp.float32)
    for part_ in range(4):
        for jq in range(4):
            send_c[part_ * 4 + jq] = small[pl.ds(part_ * TOK + jq, 16, stride=4), :].astype(jnp.bfloat16)
    send_c[16] = small[pl.ds(16 * 16, 16), :].astype(jnp.bfloat16)

    def middle(t):
        zp = t // 2 if t < 16 else 0
        xp = (t % 2) * 2 + zp % 2 if t < 16 else 1
        c = 0 if t < 16 else 1
        return zp % 2, (zp // 2) * 8 + xp * 2 + c

    places = [middle(t) for t in range(17)]
    middles = [a * 32 + b for a, b in places]
    mine = functools.reduce(jnp.logical_or, [me == m for m in middles])
    for t in sorted(range(17), key=lambda t: -t):
        @pl.when(me != middles[t])
        def _(t=t):
            pltpu.make_async_remote_copy(
                src_ref=send_c.at[t], dst_ref=recv_c.at[me], send_sem=c_s, recv_sem=c_r,
                device_id=(*places[t], tp), device_id_type=MESH,
            ).start()

        @pl.when(me == middles[t])
        def _(t=t):
            recv_c[me] = send_c[t]

    def wait_tiles(buf, sem, count):
        some = buf.at[pl.ds(0, count)]
        pltpu.make_async_copy(some, some, sem).wait()

    def reorder(src, dst):
        wide_a[...] = src[...].reshape(1024, HEAD).astype(jnp.float32)
        for u in range(4):
            pieces = wide_a[pl.ds(u, 256, stride=4), :].astype(jnp.bfloat16)
            wide_b[pl.ds(u, 256, stride=4), :] = jnp.dot(pick[...], pieces, preferred_element_type=jnp.float32)
        dst[...] = wide_b[...].astype(jnp.bfloat16).reshape(HOLDERS, 16, HEAD)

    arrived(recv_a, a_r)
    reorder(recv_a, send_b)
    spread(send_b, recv_b, b_s, b_r)

    @pl.when(mine)
    def _():
        wait_tiles(recv_c, c_r, HOLDERS - 1)
        reorder(recv_c, send_d)
        tile = jnp.where(core == 1, 16, 2 * z + x // 2)
        for dx in (2, 1, 3, 0):
            for dz in (4, 3, 5, 2, 6, 1, 7, 0):
                for o in (False, True):
                    if dz or dx or o:
                        to = device(dx=dx, dz=dz, other=o)
                        pltpu.make_async_remote_copy(
                            src_ref=send_d.at[to[0] * 32 + to[1]], dst_ref=recv_d.at[tile], send_sem=d_s, recv_sem=d_r,
                            device_id=to, device_id_type=MESH,
                        ).start()
        recv_d[tile] = send_d[me]

    arrived(recv_b, b_r)
    wide_a[...] = recv_b[...].reshape(1024, HEAD).astype(jnp.float32)
    for kv in range(2):
        for n in range(SEQ):
            for g in range(GROUP):
                old[kv, n, g * STEPS : (g + 1) * STEPS, :] = wide_a[
                    pl.ds((kv * 2 + g % 2) * 256 + n * 4 + g // 2, 16, stride=16), :
                ].astype(jnp.bfloat16)

    @pl.when(mine)
    def _():
        wait_tiles(recv_d, d_r, 16)
        wait_tiles(send_c, c_s, 16)
        wait_tiles(send_d, d_s, HOLDERS - 1)

    @pl.when(jnp.logical_not(mine))
    def _():
        wait_tiles(recv_d, d_r, 17)
        wait_tiles(send_c, c_s, 17)

    small[...] = recv_d[...].reshape(17 * 16, HEAD).astype(jnp.float32)
    owner = (lax.broadcasted_iota(jnp.int32, (TOK, HEAD), 0) // 4) % 4
    eye = lax.broadcasted_iota(jnp.int32, (128, 128), 0) == lax.broadcasted_iota(jnp.int32, (128, 128), 1)
    for kv in range(2):
        new_w = small[pl.ds(kv * TOK, TOK), :]
        new_v = small[pl.ds((2 + kv) * TOK, TOK), :].astype(jnp.bfloat16)
        for n in range(SEQ):
            share = jnp.broadcast_to(small[pl.ds(16 * 16 + n * 4 + kv, 1), :], (128, 128))
            value = jnp.dot(jnp.where(eye, share, 0.0).astype(jnp.bfloat16), old[kv, n], preferred_element_type=jnp.float32)
            value += lax.dot_general(
                jnp.where(owner == n, new_w, 0.0).astype(jnp.bfloat16), new_v, (((0,), (0,)), ((), ())),
                preferred_element_type=jnp.float32,
            )
            value = value.astype(jnp.bfloat16)
            for g in range(GROUP):
                col = (kv * GROUP + g) * HEAD
                out[n * STEPS : (n + 1) * STEPS, col : col + HEAD] = value[g * STEPS : (g + 1) * STEPS]
    for copy in started:
        copy.wait_send()
    arrived(send_a, a_s)
    arrived(send_b, b_s)


def shards(
    w_key, w_value, hidden, queries, key_cache, value_cache, prompt_lengths, rollout_lengths, batch_slots
):
    bf, f32 = jnp.bfloat16, jnp.float32
    vm, dma = pltpu.VMEM, pltpu.SemaphoreType.DMA
    hbm = pl.BlockSpec(memory_space=pl.ANY)
    smem = pl.BlockSpec(memory_space=pltpu.SMEM)
    vmem = pl.BlockSpec(memory_space=pltpu.VMEM)
    scratch = [
        vm((NY, 2, 32, 256), bf),
        vm((NX, TOK, 512), bf),
        vm((NY, 2 * NX * TOK, 512), bf),
        vm((NZ, 2, 128, 256), bf),
        vm((TOK, 2048), bf),
        vm((SEQ * CTX, 256), bf),
        vm((SEQ * CTX, 256), bf),
        vm((2, NX, TOK, 256), f32),
        vm((2, NX, TOK, 256), bf),
        vm((2, NX, TOK, 256), bf),
        vm((2, TOK, 256), bf),
        vm((2, 512, HEAD), bf),
        vm((2, 512, HEAD), f32),
        vm((2 * SEQ, 8, HEAD), f32),
        vm((2 * SEQ, 8, HEAD), f32),
        vm((256, 256), bf),
    ]
    scratch += [vm((HOLDERS, 16, HEAD), bf)] * 4 + [vm((1024, HEAD), f32)] * 2
    scratch += [vm((17, 16, HEAD), bf), vm((HOLDERS, 16, HEAD), bf)] * 2 + [vm((17 * 16, HEAD), f32), vm((2, SEQ, 128, HEAD), bf)]
    scratch += [dma((21,))]
    scratch += [dma((4, 2))] * 2 + [dma((3,))] * 2
    scratch += [dma((4,))] * 6 + [dma((4, 4))] * 2
    scratch += [dma((4, 4))] * 4
    scratch += [dma((2, 4))] * 2
    scratch += [dma] * 8
    result = pl.pallas_call(
        kernel,
        out_shape=jax.ShapeDtypeStruct((TOK, 2048), bf),
        in_specs=[smem, smem, vmem] + [hbm] * 6,
        out_specs=vmem,
        scratch_shapes=scratch,
        compiler_params=pltpu.CompilerParams(collective_id=0, has_side_effects=True, vmem_limit_bytes=60 * 1024 * 1024),
        name="rollout",
    )(
        prompt_lengths,
        rollout_lengths,
        batch_slots.reshape(1, 256),
        w_key,
        w_value,
        hidden.reshape(TOK, 2048),
        queries.reshape(TOK, 2048),
        key_cache.reshape(SEQ * CTX, 256),
        value_cache.reshape(SEQ * CTX, 256),
    )
    return result.reshape(SEQ, STEPS, 2048)


def solution(mesh):
    rows = P(("sect", "dp", "tp"), None)
    spread = P(("sect", "dp"), None, "tp")
    each = P(("sect", "dp"))
    return jax.shard_map(
        shards,
        mesh=mesh,
        in_specs=(rows, rows, spread, spread, spread, spread, each, each, P()),
        out_specs=spread,
        check_vma=False,
    )
```

```python
import functools

import jax
import jax.numpy as jnp
from jax import lax
from jax.experimental import pallas as pl
from jax.experimental.pallas import tpu as pltpu
from jax.sharding import PartitionSpec as P

MESH = pl.DeviceIdType.MESH
HEAD = 128
STEPS = 16
CTX = 512
GROUP = 8
SEQ = 4
TOK = SEQ * STEPS
NX, NY, NZ = 4, 4, 8
HOLDERS = 64
LOG2E = 1.4426950408889634
NEG = -1e30
FIRST = [(1,), (1,), (1,), (1,)]
ONWARD = [{1: (1,), 2: (1, 2)}] * 4
GREET = (-1, 1)
STRAIGHT = ()
SLANTED = (1, 3)


def kernel(
    lens, rolls, slots, w_key, w_value, hidden, queries, key_cache, value_cache, out,
    w_stage, h_stage, acts, weights, qs, kc, vc, part, part_send, part_recv, fresh, qrows, oc, mc, lc, pick,
    send_a, recv_a, send_b, recv_b, wide_a, wide_b, send_c, recv_c, recv_d, send_d, small, old,
    loc, w1s, w1r, h1s, h1r, ups, upr, dns, dnr, hfs, hfr, hxs, hxr,
    zus, zur, zds, zdr, rs, rr, a_s, a_r, b_s, b_r, c_s, c_r, d_s, d_r,
):
    sect, dp, tp = lax.axis_index("sect"), lax.axis_index("dp"), lax.axis_index("tp")
    z_hi, x, core = dp // 8, (dp // 2) % 4, dp % 2
    z = 2 * z_hi + sect
    me = sect * 32 + dp

    def at_z(d):
        return (z + d + NZ) % NZ

    def block(zp):
        return (zp % 2) * 4 + zp // 2

    def device(dx=0, dy=0, dz=0, other=False):
        zp = at_z(dz)
        c = 1 - core if other else core
        return (zp % 2, (zp // 2) * 8 + ((x + dx + NX) % NX) * 2 + c, (tp + dy + NY) % NY)

    started = []

    def send(src, dst, s_sem, r_sem, to):
        copy = pltpu.make_async_remote_copy(
            src_ref=src, dst_ref=dst, send_sem=s_sem, recv_sem=r_sem, device_id=to, device_id_type=MESH
        )
        copy.start()
        started.append(copy)
        return copy

    def local(src, dst, sem):
        copy = pltpu.make_async_copy(src, dst, sem)
        copy.start()
        return copy

    zz = block(z)
    rows_w = pl.ds(pl.multiple_of(tp * 32, 32), 32)
    there = 1 - core

    def tokens(xp, c):
        return pl.ds(pl.multiple_of((c * NX + xp) * TOK, TOK), TOK)

    partners = [device(dx=k, other=o) for k in range(1, NX) for o in (False, True)]
    partners += [device(dy=k, other=o) for k in range(1, NY) for o in (False, True)] + [device(other=True)]
    partners += [device(dz=k) for k in GREET] + [device(dx=k, dy=d) for k in SLANTED for d in (-1, 1)]
    barrier = pltpu.get_barrier_semaphore()
    for partner in partners:
        pl.semaphore_signal(barrier, inc=1, device_id=partner, device_id_type=MESH)
    own_q = [local(queries, qs, loc.at[0]), local(key_cache, kc, loc.at[1]), local(value_cache, vc, loc.at[2])]
    staged = [
        local(src.at[:, y * 256 : y * 256 + 256], w_stage.at[y, b], loc.at[3 + y * 2 + b])
        for y in range(NY)
        for b, src in enumerate((w_key, w_value))
    ]
    staged += [
        local(
            hidden.at[:, b * 1024 + xp * 256 : b * 1024 + xp * 256 + 256],
            h_stage.at[xp, :, b * 256 : b * 256 + 256],
            loc.at[11 + xp * 2 + b],
        )
        for xp in range(NX)
        for b in range(2)
    ]
    pl.semaphore_wait(barrier, len(partners))
    for copy in staged:
        copy.wait()

    w1 = {}

    def wsend(k, o):
        w1[k, o] = send(
            w_stage.at[(tp + k) % NY, there if o else core], weights.at[zz, core, rows_w, :],
            w1s.at[k, o], w1r.at[k, o], device(dy=k, other=o == 1),
        )

    up, down = {}, {}

    def piece(d, k):
        rows = pl.ds(pl.multiple_of(((tp - k + NY) % NY) * 32, 32), 32)
        return weights.at[block(at_z(d)), :, rows, :]

    def zsend(k, dist, hop=1):
        if dist < 4 or k < 2:
            ref = piece(hop - dist, k)
            up[k, dist] = [send(ref, ref, zus.at[k, dist - 1], zur.at[k, dist - 1], device(dz=hop))]
        if dist < 4 or k >= 2:
            ref = piece(dist - hop, k)
            down[k, dist] = [send(ref, ref, zds.at[k, dist - 1], zdr.at[k, dist - 1], device(dz=-hop))]

    def zfirst(k):
        for dist in FIRST[k]:
            zsend(k, dist, dist)

    def zpass(k, dist):
        for copy in up.get((k, dist), []) + down.get((k, dist), []):
            copy.wait_recv()
        for hop in ONWARD[k].get(dist, ()):
            zsend(k, dist + hop, hop)

    h1, hup, hdn, hfar, hx = {}, {}, {}, {}, {}

    def hsend(k):
        h1[k] = send(
            h_stage.at[(x + k) % NX], acts.at[tp, tokens(x, core), :], h1s.at[k - 1], h1r.at[k - 1], device(dx=k)
        )
        if k in SLANTED:
            src, dst = h_stage.at[(x + k) % NX], acts.at[tp, tokens(x, core), :]
            hup[k] = send(src, dst, ups.at[k], upr.at[k], device(dx=k, dy=1))
            hdn[k] = send(src, dst, dns.at[k], dnr.at[k], device(dx=k, dy=-1))


    def chunk(dy, k):
        return acts.at[(tp + dy + NY) % NY, tokens((x - k + NX) % NX, core), :]

    def hcore(dy, k):
        ref = chunk(dy, k)
        hx[dy, k] = send(ref, ref, hxs.at[dy % NY, k], hxr.at[dy % NY, k], device(other=True))

    def ysend(k):
        ref = chunk(0, k)
        if k not in SLANTED:
            hup[k] = send(ref, ref, ups.at[k], upr.at[k], device(dy=1))
            hdn[k] = send(ref, ref, dns.at[k], dnr.at[k], device(dy=-1))
        if k in STRAIGHT:
            hfar[k] = send(ref, ref, hfs.at[k], hfr.at[k], device(dy=2))
        hcore(0, k)

    def yforward(k):
        if k % 2 == 0:
            hup[k].wait_recv()
            ref = chunk(-1, k)
            if k not in STRAIGHT:
                hfar[k] = send(ref, ref, hfs.at[k], hfr.at[k], device(dy=1))
            hcore(-1, k)
        else:
            hdn[k].wait_recv()
            ref = chunk(1, k)
            if k not in STRAIGHT:
                hfar[k] = send(ref, ref, hfs.at[k], hfr.at[k], device(dy=-1))
            hcore(1, k)

    def yother(k):
        if k % 2 == 0:
            hdn[k].wait_recv()
            hcore(1, k)
        else:
            hup[k].wait_recv()
            hcore(-1, k)

    def ylast(k):
        hfar[k].wait_recv()
        hcore(2, k)

    for k in (2, 1, 3, 0):
        for o in range(2):
            if k or o:
                wsend(k, o)
    own = [local(w_stage.at[tp, core], weights.at[zz, core, rows_w, :], loc.at[19])]
    own += [local(h_stage.at[x], acts.at[tp, tokens(x, core), :], loc.at[20])]
    for k in (2, 1, 3):
        hsend(k)
    own[1].wait()
    ysend(0)
    own[0].wait()
    w1[0, 1].wait_recv()
    zfirst(0)

    scale = HEAD ** (-0.5) * LOG2E

    def over_cache(n, kv):
        q = jnp.concatenate(
            [qs[n * STEPS : (n + 1) * STEPS, (kv * GROUP + g) * HEAD : (kv * GROUP + g + 1) * HEAD] for g in range(GROUP)],
            axis=0,
        )
        rows = slice(n * 128, (n + 1) * 128)
        qrows[kv, rows, :] = q
        keys = kc[n * CTX : (n + 1) * CTX, kv * HEAD : (kv + 1) * HEAD]
        vals = vc[n * CTX : (n + 1) * CTX, kv * HEAD : (kv + 1) * HEAD]
        score = lax.dot_general(q, keys, (((1,), (1,)), ((), ())), preferred_element_type=jnp.float32)
        live = lax.broadcasted_iota(jnp.int32, (128, CTX), 1) < lens[n]
        score = jnp.where(live, score * scale, NEG)
        top = jnp.max(score, axis=1, keepdims=True)
        e = jnp.exp2(score - top)
        total = jnp.sum(e, axis=1, keepdims=True)
        value = jnp.dot(e.astype(jnp.bfloat16), vals, preferred_element_type=jnp.float32)
        oc[kv, rows, :] = value / total
        mc[kv * SEQ + n, :, :] = jnp.transpose(jnp.broadcast_to(top, (128, HEAD)))[:8]
        lc[kv * SEQ + n, :, :] = jnp.transpose(jnp.broadcast_to(total, (128, HEAD)))[:8]

    def spread(src, dst, s_sem, r_sem, columns=(2, 1, 3, 0)):
        for dx in columns:
            for dz in (4, 3, 5, 2, 6, 1, 7, 0):
                for o in (False, True):
                    if dz or dx or o:
                        to = device(dx=dx, dz=dz, other=o)
                        pltpu.make_async_remote_copy(
                            src_ref=src.at[to[0] * 32 + to[1]], dst_ref=dst.at[me], send_sem=s_sem, recv_sem=r_sem,
                            device_id=to, device_id_type=MESH,
                        ).start()
        if 0 in columns:
            dst[me] = src[me]

    def arrived(buf, sem):
        some = buf.at[pl.ds(0, HOLDERS - 1)]
        pltpu.make_async_copy(some, some, sem).wait()

    row = lax.broadcasted_iota(jnp.int32, (256, 256), 0)
    pick[...] = jnp.where(row == slots[...], 1.0, 0.0).astype(jnp.bfloat16)

    for copy in own_q:
        copy.wait()
    over_cache(0, 0)
    over_cache(1, 0)
    over_cache(2, 0)
    over_cache(3, 0)

    def wfirst(k):
        for o in range(2):
            w1[k, o].wait_recv()
        zfirst(k)

    def hfirst(k):
        h1[k].wait_recv()
        ysend(k)

    def tiles(kv):
        for q in range(32):
            send_a[kv * 32 + q] = oc[kv, pl.ds(q, 16, stride=32), :].astype(jnp.bfloat16)

    wfirst(1)
    wfirst(3)
    zpass(0, 1)
    wfirst(2)
    hfirst(1)
    hfirst(3)
    yforward(0)
    hfirst(2)
    zpass(1, 1)
    zpass(3, 1)
    yother(0)
    zpass(0, 2)
    zpass(2, 1)
    yforward(1)
    yforward(3)
    yforward(2)
    tiles(0)
    over_cache(0, 1)
    over_cache(1, 1)
    zpass(1, 2)
    zpass(3, 2)
    for k in (1, 3, 2):
        yother(k)
    zpass(0, 3)
    zpass(2, 2)
    over_cache(2, 1)
    over_cache(3, 1)
    tiles(1)
    for k in (0, 1, 3, 2):
        ylast(k)
    zpass(0, 4)
    for k in (1, 3, 2):
        zpass(k, 3)
    for k in (1, 3, 2):
        zpass(k, 4)
    for copy in hx.values():
        copy.wait_recv()

    spread(send_a, recv_a, a_s, a_r)
    total = None
    for y in range(NY):
        term = jnp.dot(
            acts[y], weights[2 * y : 2 * y + 2].reshape(512, 256), preferred_element_type=jnp.float32
        )
        total = term if total is None else total + term
    part[...] = total.reshape(2, NX, TOK, 256)
    part_send[...] = total.reshape(2, NX, TOK, 256).astype(jnp.bfloat16)
    sums = [
        send(
            part_send.at[there if o else core, (x + k) % NX], part_recv.at[o, k],
            rs.at[o, k], rr.at[o, k], device(dx=k, other=o == 1),
        )
        for k in (2, 1, 3, 0)
        for o in range(2)
        if k or o
    ]
    for copy in sums:
        copy.wait_recv()
    same, cross = part[core, x], part_recv[1, 0].astype(jnp.float32)
    for k in range(1, NX):
        same = same + part_recv[0, k].astype(jnp.float32)
        cross = cross + part_recv[1, k].astype(jnp.float32)
    fresh[core] = same.astype(jnp.bfloat16)
    fresh[there] = cross.astype(jnp.bfloat16)

    r = lax.broadcasted_iota(jnp.int32, (STEPS, 128), 1) % STEPS
    seen = lax.broadcasted_iota(jnp.int32, (STEPS, 128), 0) <= r
    small[16 * 16 :, :] = jnp.zeros((16, HEAD), jnp.float32)
    for kv in range(2):
        for n in range(SEQ):
            keys = fresh[0, n * STEPS : (n + 1) * STEPS, kv * HEAD : (kv + 1) * HEAD]
            score = lax.dot_general(
                keys, qrows[kv, n * 128 : (n + 1) * 128, :], (((1,), (1,)), ((), ())),
                preferred_element_type=jnp.float32,
            )
            score = jnp.where(seen, score * scale, NEG)
            before = mc[kv * SEQ + n, 0:1, :]
            top = jnp.maximum(before, jnp.max(score, axis=0, keepdims=True))
            e = jnp.exp2(score - top)
            cached = lc[kv * SEQ + n, 0:1, :] * jnp.exp2(before - top)
            factor = 1.0 / (cached + jnp.sum(e, axis=0, keepdims=True))
            factor = jnp.where(r[0:1, :] < rolls[n], factor, 0.0)
            small[pl.ds(kv * TOK + n * STEPS, STEPS), :] = e * factor
            small[pl.ds(16 * 16 + n * 4 + kv, 1), :] = cached * factor
        small[pl.ds((2 + kv) * TOK, TOK), :] = fresh[1, :, kv * HEAD : (kv + 1) * HEAD].astype(jnp.float32)
    for part_ in range(4):
        for jq in range(4):
            send_c[part_ * 4 + jq] = small[pl.ds(part_ * TOK + jq, 16, stride=4), :].astype(jnp.bfloat16)
    send_c[16] = small[pl.ds(16 * 16, 16), :].astype(jnp.bfloat16)

    def middle(t):
        zp = t // 2 if t < 16 else 0
        xp = (t % 2) * 2 + zp % 2 if t < 16 else 1
        c = 0 if t < 16 else 1
        return zp % 2, (zp // 2) * 8 + xp * 2 + c

    places = [middle(t) for t in range(17)]
    middles = [a * 32 + b for a, b in places]
    mine = functools.reduce(jnp.logical_or, [me == m for m in middles])
    for t in sorted(range(17), key=lambda t: -t):
        @pl.when(me != middles[t])
        def _(t=t):
            pltpu.make_async_remote_copy(
                src_ref=send_c.at[t], dst_ref=recv_c.at[me], send_sem=c_s, recv_sem=c_r,
                device_id=(*places[t], tp), device_id_type=MESH,
            ).start()

        @pl.when(me == middles[t])
        def _(t=t):
            recv_c[me] = send_c[t]

    def wait_tiles(buf, sem, count):
        some = buf.at[pl.ds(0, count)]
        pltpu.make_async_copy(some, some, sem).wait()

    def reorder(src, dst):
        wide_a[...] = src[...].reshape(1024, HEAD).astype(jnp.float32)
        for u in range(4):
            pieces = wide_a[pl.ds(u, 256, stride=4), :].astype(jnp.bfloat16)
            wide_b[pl.ds(u, 256, stride=4), :] = jnp.dot(pick[...], pieces, preferred_element_type=jnp.float32)
        dst[...] = wide_b[...].astype(jnp.bfloat16).reshape(HOLDERS, 16, HEAD)

    arrived(recv_a, a_r)
    reorder(recv_a, send_b)
    spread(send_b, recv_b, b_s, b_r)

    @pl.when(mine)
    def _():
        wait_tiles(recv_c, c_r, HOLDERS - 1)
        reorder(recv_c, send_d)
        tile = jnp.where(core == 1, 16, 2 * z + x // 2)
        for dx in (2, 1, 3, 0):
            for dz in (4, 3, 5, 2, 6, 1, 7, 0):
                for o in (False, True):
                    if dz or dx or o:
                        to = device(dx=dx, dz=dz, other=o)
                        pltpu.make_async_remote_copy(
                            src_ref=send_d.at[to[0] * 32 + to[1]], dst_ref=recv_d.at[tile], send_sem=d_s, recv_sem=d_r,
                            device_id=to, device_id_type=MESH,
                        ).start()
        recv_d[tile] = send_d[me]

    arrived(recv_b, b_r)
    wide_a[...] = recv_b[...].reshape(1024, HEAD).astype(jnp.float32)
    for kv in range(2):
        for n in range(SEQ):
            for g in range(GROUP):
                old[kv, n, g * STEPS : (g + 1) * STEPS, :] = wide_a[
                    pl.ds((kv * 2 + g % 2) * 256 + n * 4 + g // 2, 16, stride=16), :
                ].astype(jnp.bfloat16)

    @pl.when(mine)
    def _():
        wait_tiles(recv_d, d_r, 16)
        wait_tiles(send_c, c_s, 16)
        wait_tiles(send_d, d_s, HOLDERS - 1)

    @pl.when(jnp.logical_not(mine))
    def _():
        wait_tiles(recv_d, d_r, 17)
        wait_tiles(send_c, c_s, 17)

    small[...] = recv_d[...].reshape(17 * 16, HEAD).astype(jnp.float32)
    owner = (lax.broadcasted_iota(jnp.int32, (TOK, HEAD), 0) // 4) % 4
    eye = lax.broadcasted_iota(jnp.int32, (128, 128), 0) == lax.broadcasted_iota(jnp.int32, (128, 128), 1)
    for kv in range(2):
        new_w = small[pl.ds(kv * TOK, TOK), :]
        new_v = small[pl.ds((2 + kv) * TOK, TOK), :].astype(jnp.bfloat16)
        for n in range(SEQ):
            share = jnp.broadcast_to(small[pl.ds(16 * 16 + n * 4 + kv, 1), :], (128, 128))
            value = jnp.dot(jnp.where(eye, share, 0.0).astype(jnp.bfloat16), old[kv, n], preferred_element_type=jnp.float32)
            value += lax.dot_general(
                jnp.where(owner == n, new_w, 0.0).astype(jnp.bfloat16), new_v, (((0,), (0,)), ((), ())),
                preferred_element_type=jnp.float32,
            )
            value = value.astype(jnp.bfloat16)
            for g in range(GROUP):
                col = (kv * GROUP + g) * HEAD
                out[n * STEPS : (n + 1) * STEPS, col : col + HEAD] = value[g * STEPS : (g + 1) * STEPS]
    for copy in started:
        copy.wait_send()
    arrived(send_a, a_s)
    arrived(send_b, b_s)


def shards(
    w_key, w_value, hidden, queries, key_cache, value_cache, prompt_lengths, rollout_lengths, batch_slots
):
    bf, f32 = jnp.bfloat16, jnp.float32
    vm, dma = pltpu.VMEM, pltpu.SemaphoreType.DMA
    hbm = pl.BlockSpec(memory_space=pl.ANY)
    smem = pl.BlockSpec(memory_space=pltpu.SMEM)
    vmem = pl.BlockSpec(memory_space=pltpu.VMEM)
    scratch = [
        vm((NY, 2, 32, 256), bf),
        vm((NX, TOK, 512), bf),
        vm((NY, 2 * NX * TOK, 512), bf),
        vm((NZ, 2, 128, 256), bf),
        vm((TOK, 2048), bf),
        vm((SEQ * CTX, 256), bf),
        vm((SEQ * CTX, 256), bf),
        vm((2, NX, TOK, 256), f32),
        vm((2, NX, TOK, 256), bf),
        vm((2, NX, TOK, 256), bf),
        vm((2, TOK, 256), bf),
        vm((2, 512, HEAD), bf),
        vm((2, 512, HEAD), f32),
        vm((2 * SEQ, 8, HEAD), f32),
        vm((2 * SEQ, 8, HEAD), f32),
        vm((256, 256), bf),
    ]
    scratch += [vm((HOLDERS, 16, HEAD), bf)] * 4 + [vm((1024, HEAD), f32)] * 2
    scratch += [vm((17, 16, HEAD), bf), vm((HOLDERS, 16, HEAD), bf)] * 2 + [vm((17 * 16, HEAD), f32), vm((2, SEQ, 128, HEAD), bf)]
    scratch += [dma((21,))]
    scratch += [dma((4, 2))] * 2 + [dma((3,))] * 2
    scratch += [dma((4,))] * 6 + [dma((4, 4))] * 2
    scratch += [dma((4, 4))] * 4
    scratch += [dma((2, 4))] * 2
    scratch += [dma] * 8
    result = pl.pallas_call(
        kernel,
        out_shape=jax.ShapeDtypeStruct((TOK, 2048), bf),
        in_specs=[smem, smem, vmem] + [hbm] * 6,
        out_specs=vmem,
        scratch_shapes=scratch,
        compiler_params=pltpu.CompilerParams(collective_id=0, has_side_effects=True, vmem_limit_bytes=60 * 1024 * 1024),
        name="rollout",
    )(
        prompt_lengths,
        rollout_lengths,
        batch_slots.reshape(1, 256),
        w_key,
        w_value,
        hidden.reshape(TOK, 2048),
        queries.reshape(TOK, 2048),
        key_cache.reshape(SEQ * CTX, 256),
        value_cache.reshape(SEQ * CTX, 256),
    )
    return result.reshape(SEQ, STEPS, 2048)


def solution(mesh):
    rows = P(("sect", "dp", "tp"), None)
    spread = P(("sect", "dp"), None, "tp")
    each = P(("sect", "dp"))
    return jax.shard_map(
        shards,
        mesh=mesh,
        in_specs=(rows, rows, spread, spread, spread, spread, each, each, P()),
        out_specs=spread,
        check_vma=False,
    )
```
